512 devices in a mesh: seq: 16 (over x, y_hi, core), res: 32 (over y_lo, z).
Axes of the slice: x: 4, y: 4 (y_hi: 2, y_lo: 2; y = y_hi * 2 + y_lo), z: 16, core: 2. Of those that a mesh axis runs over, the one named last changes fastest.
Arguments:
- alignment_features: bfloat16 [64, 4096, 256], P('seq', 'res'), may hold values from -6 to 6
- coupling_logit_offset: bfloat16 [8, 4096, 4096], P(None, 'res', 'seq'), may hold values from -310 to 310
- contact_tile_filter: int32 [32, 32], replicated, may hold values from 0 to 1, as said below
- standard_scale_array: float32 [256], replicated, may hold values from 0.25 to 1.75
- standard_offset_array: float32 [256], replicated, may hold values from -3 to 3
- probe_projection: bfloat16 [256, 256], replicated, may hold values from -0.375 to 0.375
- lookup_projection: bfloat16 [256, 256], replicated, may hold values from -0.375 to 0.375
- content_projection: bfloat16 [256, 256], replicated, may hold values from -0.375 to 0.375
- sigmoid_projection: bfloat16 [256, 256], replicated, may hold values from -0.375 to 0.375
- sigmoid_offset_array: float32 [256], replicated, may hold values from -4 to 4
- result_projection: bfloat16 [256, 256], replicated, may hold values from -0.375 to 0.375
- result_offset: float32 [256], replicated, may hold values from -3 to 3
Outputs:
- update: bfloat16 [64, 4096, 256], P('seq', 'res')
The draws below stay inside these ranges and needn't reach their ends.
Inputs may be any that keep to these rules, and one draw needn't show every extreme that they name: `contact_tile_filter`: every diagonal entry is 1.
All inputs are finite; a program needn't handle non-finite values.
Results may differ from the reference program's by a relative error of at most 0.006.
Values may be sent and summed in bfloat16 or wider, within the bound.
No kernel may reach another device: no remote copies, remote signals or barrier semaphores. Data moves between devices by JAX's collectives and lax.ppermute only.
A program may use at most 64 MiB of HBM per device.

```python
import jax
import jax.numpy as jnp
from jax import lax

ALIGNED_FEATURES = 256
H = 8
DH = 32
BLOCK = 128
ALIGNED_DEPTH = 64
AMINO_LENGTH = 4096


def draw_coupling_logit_offset(key, part):
    key = jax.random.fold_in(key, 11)
    key_base = jax.random.fold_in(key, 0)
    result = jnp.clip(jax.random.normal(key_base, (H, AMINO_LENGTH, AMINO_LENGTH), jnp.float32), -4.0, 4.0)
    return result.astype(jnp.bfloat16)


def draw_contact_tile_filter(key, part):
    key = jax.random.fold_in(key, 23)
    key_density, key_entry = jax.random.split(key)
    block_count = AMINO_LENGTH // BLOCK
    density = jax.random.randint(key_density, (block_count, 1), 1, 9)
    entries = jax.random.randint(key_entry, (block_count, block_count), 0, 8) < density
    diagonal = jnp.arange(block_count)[:, None] == jnp.arange(block_count)[None, :]
    return (entries | diagonal).astype(jnp.int32)


def block_levels(own_key, extent, pieces, smallest, top_value):
    def one(position, blocks):
        draws = jax.random.uniform(jax.random.fold_in(jax.random.fold_in(own_key, 6), position), (blocks,), jnp.float32, smallest / len(pieces), top_value / len(pieces))
        return jnp.repeat(jnp.exp(draws), extent[position] // blocks).reshape((-1,) + (1,) * (len(extent) - position - 1))

    level = one(*pieces[0])
    for cut in pieces[1:]:
        level = level * one(*cut)
    return level


def centred(key, dims, scale, reach, pieces=(), kind=jnp.bfloat16):
    factor_of = block_levels(key, dims, pieces, -0.22, 0.18) if pieces else 1.0
    values = jax.random.normal(key, dims, jnp.float32) * scale * factor_of
    return jnp.minimum(jnp.maximum(values, -reach), reach).astype(kind)


def setup_inputs(seed: int = 0) -> dict:
    seeds = jax.random.split(jax.random.key(seed), 13)
    alignment_features = centred(seeds[0], (ALIGNED_DEPTH, AMINO_LENGTH, ALIGNED_FEATURES), 1.0, 6.0, ((0, 16), (1, 32)))
    coupling_logit_offset = draw_coupling_logit_offset(jax.random.fold_in(seeds[12], 71), 0)
    contact_tile_filter = draw_contact_tile_filter(jax.random.fold_in(seeds[12], 71), 0)
    standard_scale_array = jnp.clip(1.0 + 0.15 * jax.random.normal(seeds[3], (ALIGNED_FEATURES,), jnp.float32), 0.25, 1.75)
    standard_offset_array = centred(seeds[4], (ALIGNED_FEATURES,), 0.5, 3.0, (), jnp.float32)
    probe_projection = centred(seeds[5], (ALIGNED_FEATURES, ALIGNED_FEATURES), ALIGNED_FEATURES ** -0.5, 0.375)
    lookup_projection = centred(seeds[6], (ALIGNED_FEATURES, ALIGNED_FEATURES), ALIGNED_FEATURES ** -0.5, 0.375)
    content_projection = centred(seeds[7], (ALIGNED_FEATURES, ALIGNED_FEATURES), ALIGNED_FEATURES ** -0.5, 0.375)
    sigmoid_projection = centred(seeds[8], (ALIGNED_FEATURES, ALIGNED_FEATURES), ALIGNED_FEATURES ** -0.5, 0.375)
    sigmoid_offset_array = centred(seeds[9], (ALIGNED_FEATURES,), 1.0, 4.0, (), jnp.float32)
    result_projection = centred(seeds[10], (ALIGNED_FEATURES, ALIGNED_FEATURES), ALIGNED_FEATURES ** -0.5, 0.375)
    result_offset = centred(seeds[11], (ALIGNED_FEATURES,), 0.5, 3.0, (), jnp.float32)
    return dict(alignment_features=alignment_features, coupling_logit_offset=coupling_logit_offset, contact_tile_filter=contact_tile_filter, standard_scale_array=standard_scale_array, standard_offset_array=standard_offset_array, probe_projection=probe_projection, lookup_projection=lookup_projection, content_projection=content_projection, sigmoid_projection=sigmoid_projection, sigmoid_offset_array=sigmoid_offset_array, result_projection=result_projection, result_offset=result_offset)


def standardize_features(source, standard_scale_array, standard_offset_array):
    values_f = source.astype(jnp.float32)
    center = lax.optimization_barrier(jnp.mean(values_f, axis=-1, keepdims=True))
    spread = lax.optimization_barrier(jnp.mean((values_f - center) ** 2, axis=-1, keepdims=True))
    return (values_f - center) * lax.rsqrt(spread + 1e-05) * standard_scale_array + standard_offset_array

def reference(alignment_features, coupling_logit_offset, contact_tile_filter, standard_scale_array, standard_offset_array, probe_projection, lookup_projection, content_projection, sigmoid_projection, sigmoid_offset_array, result_projection, result_offset):
    alignment_depth, amino_length, feature_width = alignment_features.shape
    standardized_features = standardize_features(alignment_features, standard_scale_array, standard_offset_array).astype(jnp.bfloat16)
    flat_rows = standardized_features.reshape(-1, feature_width)
    queries = (jnp.dot(flat_rows, probe_projection, preferred_element_type=jnp.float32) * (1.0 / DH ** 0.5)).astype(jnp.bfloat16)
    queries = queries.reshape(alignment_depth, amino_length, H, DH)
    key_rows = jnp.dot(flat_rows, lookup_projection, preferred_element_type=jnp.float32).astype(jnp.bfloat16).reshape(alignment_depth, amino_length, H, DH)
    value_rows = jnp.dot(flat_rows, content_projection, preferred_element_type=jnp.float32).astype(jnp.bfloat16).reshape(alignment_depth, amino_length, H, DH)
    gate_val = jax.nn.sigmoid(jnp.dot(flat_rows, sigmoid_projection, preferred_element_type=jnp.float32) + sigmoid_offset_array)
    block_count = amino_length // BLOCK

    def one_block(block_idx):
        first = (block_idx * BLOCK).astype(jnp.int32)
        query_block = lax.dynamic_slice_in_dim(queries, first, BLOCK, 1)
        bias_block = lax.dynamic_slice_in_dim(coupling_logit_offset, first, BLOCK, 1).astype(jnp.float32)
        mask_line = lax.dynamic_slice_in_dim(contact_tile_filter, block_idx.astype(jnp.int32), 1, 0)[0]
        live_cols = jnp.repeat(mask_line, BLOCK) > 0

        def one_seq(operands):
            query_seq, key_seq, value_seq = operands
            scores = jnp.einsum('ihd,jhd->hij', query_seq.astype(jnp.float32), key_seq.astype(jnp.float32)) + bias_block
            scores = jnp.where(live_cols[None, None, :], scores, -1000000000.0)
            top_score = lax.optimization_barrier(jnp.max(scores, axis=-1, keepdims=True))
            weights_exp = jnp.exp(scores - top_score)
            totals = lax.optimization_barrier(jnp.sum(weights_exp, axis=-1))
            weight_b = weights_exp.astype(jnp.bfloat16)
            summed = jnp.einsum('hij,jhd->hid', weight_b.astype(jnp.float32), value_seq.astype(jnp.float32))
            return (summed / totals[..., None]).transpose(1, 0, 2)
        return lax.map(one_seq, (query_block, key_rows, value_rows))
    blocks_out = lax.map(one_block, jnp.arange(block_count, dtype=jnp.int32))
    attended = blocks_out.transpose(1, 0, 2, 3, 4).reshape(alignment_depth * amino_length, feature_width)
    gated = (gate_val * attended).astype(jnp.bfloat16)
    result = jnp.dot(gated, result_projection, preferred_element_type=jnp.float32) + result_offset
    return result.astype(jnp.bfloat16).reshape(alignment_depth, amino_length, feature_width)
```

```python
import jax
import jax.numpy as jnp
import numpy as np
from jax import lax
from jax.experimental import pallas as pl
from jax.experimental.pallas import tpu as pltpu
from jax.sharding import PartitionSpec as P

H = 8
DH = 32
BLOCK = 128
PAIRS = H // 2
VROWS = 2 * DH + 16
LOG2E = 1.4426950408889634
LOW = -1e30

SEQ, RES, NZ = 16, 32, 16
Z_GROUPS = [[yl * NZ + z for z in range(NZ)] for yl in range(2)]
YL_PAIRS = [(r, (r + NZ) % RES) for r in range(RES)]
C_PAIRS = [(s, s ^ 1) for s in range(SEQ)]


def bias_pairs(u, v):
    pairs = []
    for x in range(4):
        for yh in range(2):
            for c in range(2):
                for yl in range(2):
                    for z in range(NZ):
                        to_x, to_yh, to_yl = (x + 2 * yl + u) % 4, yh ^ v, x // 2
                        source = (x * 4 + yh * 2 + c) * RES + yl * NZ + z
                        target = (to_x * 4 + to_yh * 2 + c) * RES + to_yl * NZ + z
                        pairs.append((source, target))
    return pairs


def standardize_features(source, standard_scale_array, standard_offset_array):
    values_f = source.astype(jnp.float32)
    center = jnp.mean(values_f, axis=-1, keepdims=True)
    spread = jnp.mean((values_f - center) ** 2, axis=-1, keepdims=True)
    return (values_f - center) * lax.rsqrt(
        spread + 1e-05
    ) * standard_scale_array + standard_offset_array


def project_kernel(rows_ref, key_w_ref, value_wt_ref, key_ref, value_ref):
    depth, span, width = rows_ref.shape[1:]
    rows = rows_ref[0].reshape(depth * span, width)
    key_ref[0] = (
        jnp.dot(rows, key_w_ref[...], preferred_element_type=jnp.float32)
        .astype(jnp.bfloat16)
        .reshape(depth, span, width)
    )
    values = lax.dot_general(
        value_wt_ref[...], rows, (((1,), (1,)), ((), ())), preferred_element_type=jnp.float32
    ).astype(jnp.bfloat16)
    ones = jnp.ones((VROWS - 2 * DH, span), jnp.bfloat16)
    for s in range(depth):
        for p in range(PAIRS):
            value_ref[0, s, p, : 2 * DH] = values[
                p * 2 * DH : (p + 1) * 2 * DH, s * span : (s + 1) * span
            ]
            value_ref[0, s, p, 2 * DH :] = ones


def project(gathered, key_w, value_wt):
    blocks, depth, span, width = gathered.shape
    return pl.pallas_call(
        project_kernel,
        grid=(blocks,),
        in_specs=[
            pl.BlockSpec((1, depth, span, width), lambda b: (b, 0, 0, 0)),
            pl.BlockSpec((width, width), lambda b: (0, 0)),
            pl.BlockSpec((width, width), lambda b: (0, 0)),
        ],
        out_specs=[
            pl.BlockSpec((1, depth, span, width), lambda b: (b, 0, 0, 0)),
            pl.BlockSpec((1, depth, PAIRS, VROWS, span), lambda b: (b, 0, 0, 0, 0)),
        ],
        out_shape=[
            jax.ShapeDtypeStruct((blocks, depth, span, width), jnp.bfloat16),
            jax.ShapeDtypeStruct((blocks, depth, PAIRS, VROWS, span), jnp.bfloat16),
        ],
        name="project",
    )(gathered, key_w, value_wt)


def attend_kernel(
    table_ref, key_ref, value_ref, query_ref, near_ref, far_ref, out_ref, lse_ref, top_ref, acc_ref
):
    depth = key_ref.shape[1]
    live = table_ref[3, 0]
    top_ref[...] = jnp.full_like(top_ref, LOW)
    acc_ref[...] = jnp.zeros_like(acc_ref)

    def bias_of(place):
        is_far = table_ref[1, place]
        turn = table_ref[2, place]
        row = pl.multiple_of(lax.rem(table_ref[0, place], 2) * BLOCK, BLOCK)
        near = near_ref[turn, 0, pl.ds(row, BLOCK), :].astype(jnp.float32)
        far = far_ref[turn, 0, pl.ds(row, BLOCK), :].astype(jnp.float32)
        return jnp.where(is_far > 0, far, near) * LOG2E

    def step(t, carry):
        place0, place1 = 2 * t, 2 * t + 1
        z0, z1 = table_ref[0, place0], table_ref[0, place1]
        absent = jnp.where(place1 < live, 0.0, -LOW)
        bias0, bias1 = bias_of(place0), bias_of(place1)
        for s in range(depth):
            query = query_ref[s, 0]
            score0 = jnp.dot(key_ref[z0, s], query, preferred_element_type=jnp.float32) + bias0
            score1 = jnp.dot(key_ref[z1, s], query, preferred_element_type=jnp.float32) + bias1
            old = top_ref[s]
            top = jnp.maximum(
                jnp.max(score0, axis=0, keepdims=True),
                jnp.max(score1, axis=0, keepdims=True) - absent,
            )
            top = jnp.maximum(old, top)
            top_ref[s] = top
            weight = jnp.concatenate(
                [
                    jnp.exp2(score0 - top).astype(jnp.bfloat16),
                    jnp.exp2(score1 - (top + absent)).astype(jnp.bfloat16),
                ],
                axis=0,
            )
            value = jnp.concatenate([value_ref[z0, s, 0], value_ref[z1, s, 0]], axis=1)
            acc_ref[s] = acc_ref[s] * jnp.exp2(old - top) + jnp.dot(
                value, weight, preferred_element_type=jnp.float32
            )
        return carry

    lax.fori_loop(0, (live + 1) // 2, step, 0)
    for s in range(depth):
        acc = acc_ref[s]
        total = acc[2 * DH : 2 * DH + 1]
        some = total > 0.0
        safe = jnp.where(some, total, 1.0)
        mean = acc[: 2 * DH] / safe
        lse = jnp.where(some, top_ref[s] + jnp.log2(safe), LOW)
        for e in range(2):
            lanes = slice(e * BLOCK, (e + 1) * BLOCK)
            out_ref[s, e * DH : (e + 1) * DH] = mean[e * DH : (e + 1) * DH, lanes].astype(
                out_ref.dtype
            )
            lse_ref[s, 0, e : e + 1] = lse[:, lanes]


def attend(table, keys, values, queries, near, far, out_type):
    blocks, depth, span, width = keys.shape
    turns = near.shape[0]
    return pl.pallas_call(
        attend_kernel,
        grid=(PAIRS,),
        in_specs=[
            pl.BlockSpec(memory_space=pltpu.SMEM),
            pl.BlockSpec((blocks, depth, span, 128), lambda p: (0, 0, 0, p // 2)),
            pl.BlockSpec((blocks, depth, 1, VROWS, span), lambda p: (0, 0, p, 0, 0)),
            pl.BlockSpec((depth, 1, 128, 256), lambda p: (0, p, 0, 0)),
            pl.BlockSpec((turns, 1, 256, 256), lambda p: (0, p, 0, 0)),
            pl.BlockSpec((turns, 1, 256, 256), lambda p: (0, p, 0, 0)),
        ],
        out_specs=[
            pl.BlockSpec((depth, 2 * DH, BLOCK), lambda p: (0, p, 0)),
            pl.BlockSpec((depth, 1, 2, BLOCK), lambda p: (0, p, 0, 0)),
        ],
        out_shape=[
            jax.ShapeDtypeStruct((depth, width, BLOCK), out_type),
            jax.ShapeDtypeStruct((depth, PAIRS, 2, BLOCK), jnp.float32),
        ],
        scratch_shapes=[
            pltpu.VMEM((depth, 1, 256), jnp.float32),
            pltpu.VMEM((depth, VROWS, 256), jnp.float32),
        ],
        compiler_params=pltpu.CompilerParams(vmem_limit_bytes=48 * 1024 * 1024),
        name="attend",
    )(table, keys, values, queries, near, far)


def finish_kernel(
    own_ref, own_lse_ref, got_ref, got_lse_ref, rows_ref, gate_wt_ref, gate_off_ref, out_w_ref,
    out_off_ref, out_ref,
):
    width, span = own_ref.shape[1:]
    own_lse, got_lse = own_lse_ref[0], got_lse_ref[0]
    own_part = 1.0 / (1.0 + jnp.exp2(got_lse - own_lse))
    got_part = 1.0 / (1.0 + jnp.exp2(own_lse - got_lse))

    def spread(part):
        return jnp.broadcast_to(part[:, None, :], (H, DH, span)).reshape(width, span)

    attended = own_ref[0] * spread(own_part) + got_ref[0].astype(jnp.float32) * spread(got_part)
    gate = jax.nn.sigmoid(
        lax.dot_general(
            gate_wt_ref[...], rows_ref[0], (((1,), (1,)), ((), ())),
            preferred_element_type=jnp.float32,
        )
        + gate_off_ref[...]
    )
    gated = (gate * attended).T.astype(jnp.bfloat16)
    result = jnp.dot(gated, out_w_ref[...], preferred_element_type=jnp.float32)
    out_ref[0] = (result + out_off_ref[...]).astype(jnp.bfloat16)


def finish(own, own_lse, got, got_lse, rows, gate_wt, gate_off, out_w, out_off):
    depth, width, span = own.shape
    whole = lambda s: (0, 0)
    part = lambda s: (s, 0, 0)
    return pl.pallas_call(
        finish_kernel,
        grid=(depth,),
        in_specs=[
            pl.BlockSpec((1, width, span), part),
            pl.BlockSpec((1, H, span), part),
            pl.BlockSpec((1, width, span), part),
            pl.BlockSpec((1, H, span), part),
            pl.BlockSpec((1, span, width), part),
            pl.BlockSpec((width, width), whole),
            pl.BlockSpec((width, 1), whole),
            pl.BlockSpec((width, width), whole),
            pl.BlockSpec((1, width), whole),
        ],
        out_specs=pl.BlockSpec((1, span, width), part),
        out_shape=jax.ShapeDtypeStruct((depth, span, width), jnp.bfloat16),
        name="finish",
    )(own, own_lse, got, got_lse, rows, gate_wt, gate_off, out_w, out_off)


def on_device(
    alignment_features,
    coupling_logit_offset,
    contact_tile_filter,
    standard_scale_array,
    standard_offset_array,
    probe_projection,
    lookup_projection,
    content_projection,
    sigmoid_projection,
    sigmoid_offset_array,
    result_projection,
    result_offset,
):
    depth, span, width = alignment_features.shape
    seq, res = lax.axis_index("seq"), lax.axis_index("res")
    x, yh, c = seq // 4, (seq // 2) % 2, seq % 2
    half, z_own = res // NZ, res % NZ

    normed = standardize_features(
        alignment_features, standard_scale_array, standard_offset_array
    ).astype(jnp.bfloat16)
    gathered = lax.all_gather(normed, "res", axis_index_groups=Z_GROUPS)
    partner = lax.ppermute(normed, "res", YL_PAIRS)

    turned = (
        coupling_logit_offset.reshape(PAIRS, 2, span, 2 * BLOCK)
        .transpose(0, 3, 1, 2)
        .reshape(PAIRS, 2 * BLOCK, 2 * span)
    )
    near = jnp.stack(
        [lax.ppermute(turned, ("seq", "res"), bias_pairs(u, v)) for u in range(4) for v in range(2)]
    )
    far = lax.ppermute(near, "seq", C_PAIRS)

    head_of = np.arange(128) // DH
    wanted = np.array([[(2 * p + e) % 4 for e in range(2)] for p in range(PAIRS)])
    spot = jnp.asarray(head_of[None, :, None] == wanted[:, None, :], jnp.bfloat16)

    def query_tiles(rows):
        queries = (
            jnp.dot(rows.reshape(-1, width), probe_projection, preferred_element_type=jnp.float32)
            * (LOG2E / DH**0.5)
        ).astype(jnp.bfloat16)
        turned_q = queries.reshape(depth, span, 2, 128).transpose(0, 2, 3, 1)
        twice = jnp.repeat(turned_q, 2, axis=1)
        tiles = twice[:, :, :, None, :] * spot[None, :, :, :, None]
        return tiles.reshape(depth, PAIRS, 128, 2 * span)

    places = jnp.arange(NZ, dtype=jnp.int32)

    def live_table(yl):
        line = yl * NZ + z_own
        chosen = (jnp.arange(RES, dtype=jnp.int32) == line).astype(jnp.int32)
        mask_line = jnp.sum(contact_tile_filter * chosen[:, None], axis=0).reshape(2, NZ)
        live = jnp.where(half > 0, mask_line[1], mask_line[0])
        before = jnp.sum(jnp.where(places[None, :] <= places[:, None], live[None, :], 0), axis=1) - 1
        hit = (before[:, None] == places[None, :]) & (live[:, None] > 0)
        z = jnp.sum(jnp.where(hit, places[:, None], 0), axis=0)
        slot = z // 8 + 2 * yl
        turn = ((x - 2 * half - slot) % 4) * 2 + (((z // 4) % 2) ^ yh)
        is_far = ((z // 2) % 2) ^ c
        return jnp.stack([z, is_far, turn, jnp.full((NZ,), jnp.sum(live))]).astype(jnp.int32)

    keys, values = project(gathered, lookup_projection, content_projection.T)
    sent, sent_lse = attend(
        live_table(1 - half), keys, values, query_tiles(partner), near, far, jnp.bfloat16
    )
    got = lax.ppermute(sent, "res", YL_PAIRS)
    got_lse = lax.ppermute(sent_lse, "res", YL_PAIRS)
    own, own_lse = attend(
        live_table(half), keys, values, query_tiles(normed), near, far, jnp.float32
    )
    return finish(
        own,
        own_lse.reshape(depth, H, span),
        got,
        got_lse.reshape(depth, H, span),
        normed,
        sigmoid_projection.T,
        sigmoid_offset_array[:, None],
        result_projection,
        result_offset[None, :],
    )


def solution(mesh):
    return jax.shard_map(
        on_device,
        mesh=mesh,
        in_specs=(
            P("seq", "res", None),
            P(None, "res", "seq"),
            P(),
            P(),
            P(),
            P(),
            P(),
            P(),
            P(),
            P(),
            P(),
            P(),
        ),
        out_specs=P("seq", "res", None),
        check_vma=False,
    )
```

```python
import jax
import jax.numpy as jnp
import numpy as np
from jax import lax
from jax.experimental import pallas as pl
from jax.experimental.pallas import tpu as pltpu
from jax.sharding import PartitionSpec as P

H = 8
DH = 32
BLOCK = 128
HALF = 128
GROUP = 4
TILE = 4
EXTRA = 16
SAFE_LOW = 2.0**-60
SAFE_HIGH = 2.0**90
LOG2E = 1.4426950408889634
LOW = -1e30

SEQ, RES, NZ = 16, 32, 16
Z_GROUPS = [[yl * NZ + z for z in range(NZ)] for yl in range(2)]
YL_PAIRS = [(r, (r + NZ) % RES) for r in range(RES)]
C_PAIRS = [(s, s ^ 1) for s in range(SEQ)]


def bias_pairs(u, v):
    pairs = []
    for x in range(4):
        for yh in range(2):
            for c in range(2):
                for yl in range(2):
                    for z in range(NZ):
                        to_x, to_yh, to_yl = (x + 2 * yl + u) % 4, yh ^ v, x // 2
                        source = (x * 4 + yh * 2 + c) * RES + yl * NZ + z
                        target = (to_x * 4 + to_yh * 2 + c) * RES + to_yl * NZ + z
                        pairs.append((source, target))
    return pairs


def standardize_features(source, scale, offset):
    values_f = source.astype(jnp.float32)
    center = jnp.mean(values_f, axis=-1, keepdims=True)
    spread = jnp.mean((values_f - center) ** 2, axis=-1, keepdims=True)
    return (values_f - center) * lax.rsqrt(spread + 1e-05) * scale + offset


def normalize_kernel(features_ref, scale_ref, offset_ref, out_ref):
    for s in range(features_ref.shape[0]):
        out_ref[s] = standardize_features(
            features_ref[s], scale_ref[...], offset_ref[...]
        ).astype(jnp.bfloat16)


def normalize(features, scale, offset):
    return pl.pallas_call(
        normalize_kernel,
        out_shape=jax.ShapeDtypeStruct(features.shape, jnp.bfloat16),
        name="normalize",
    )(features, scale, offset)


def prepare_kernel(
    normed_ref, partner_ref, scale_ref, offset_ref, query_w_ref, gate_w_ref, gate_off_ref,
    query_ref, gate_ref,
):
    for s in range(normed_ref.shape[0]):
        own = normed_ref[s]
        other = standardize_features(partner_ref[s], scale_ref[...], offset_ref[...]).astype(
            jnp.bfloat16
        )
        for r, rows in enumerate((other, own)):
            query = jnp.dot(rows, query_w_ref[...], preferred_element_type=jnp.float32)
            query_ref[r, s] = (query * (LOG2E / DH**0.5)).astype(jnp.bfloat16)
        gate_ref[s] = jax.nn.sigmoid(
            jnp.dot(own, gate_w_ref[...], preferred_element_type=jnp.float32) + gate_off_ref[...]
        )


def prepare(normed, partner, scale, offset, query_w, gate_w, gate_off):
    depth, span, width = normed.shape
    return pl.pallas_call(
        prepare_kernel,
        out_shape=[
            jax.ShapeDtypeStruct((2, depth, span, width), jnp.bfloat16),
            jax.ShapeDtypeStruct((depth, span, width), jnp.float32),
        ],
        name="prepare",
    )(normed, partner, scale, offset, query_w, gate_w, gate_off)


def attend_kernel(
    mask_ref, rows_ref, key_w_ref, value_w_ref, query_ref, near0_ref, near1_ref, far0_ref, far1_ref,
    sent_ref, own_ref,
    table_ref, key_ref, value_ref, spread_ref, bias_ref, acc_ref, top_ref, shift_ref,
):
    blocks, depth, span, width = rows_ref.shape
    g, r = pl.program_id(0), pl.program_id(1)
    seq, res = lax.axis_index("seq"), lax.axis_index("res")
    x, yh, c = seq // 4, lax.rem(seq // 2, 2), lax.rem(seq, 2)
    half, z_own = res // NZ, lax.rem(res, NZ)
    yl = jnp.where(r == 0, 1 - half, half)

    @pl.when((r == 0) & (g == 0))
    def _():
        key_wt = key_w_ref[...].astype(jnp.float32).T.astype(jnp.bfloat16)

        def fill(t, carry):
            rows = rows_ref[pl.ds(2 * t, 2)].reshape(2 * depth * span, width)
            keys = lax.dot_general(
                key_wt, rows, (((1,), (1,)), ((), ())), preferred_element_type=jnp.float32
            ).astype(jnp.bfloat16)
            values = jnp.dot(rows, value_w_ref[...], preferred_element_type=jnp.float32).astype(
                jnp.bfloat16
            )
            for i in range(2):
                for s in range(depth):
                    part = slice((i * depth + s) * span, (i * depth + s + 1) * span)
                    for e in range(2):
                        lanes = slice(e * HALF, (e + 1) * HALF)
                        key_ref[e, s, 2 * t + i] = keys[lanes, part]
                        value_ref[e, s, 2 * t + i, :, :HALF] = values[part, lanes]
                        value_ref[e, s, 2 * t + i, :, HALF:] = jnp.ones((span, HALF), jnp.bfloat16)
            return carry

        lax.fori_loop(0, blocks // 2, fill, 0)

    def clear(i, carry):
        for row in range(3):
            table_ref[row, i] = 0
        return carry

    def place(z, count):
        slot = z // 8 + 2 * yl
        table_ref[0, count] = z
        table_ref[1, count] = lax.rem(z // 2, 2) ^ c
        table_ref[2, count] = 2 * lax.rem(x - 2 * half - slot + 8, 4) + (lax.rem(z // 4, 2) ^ yh)
        return count + jnp.where(mask_ref[yl * NZ + z_own, half * NZ + z] > 0, 1, 0)

    lax.fori_loop(0, blocks, clear, 0)
    live = lax.fori_loop(0, blocks, place, 0)

    head_of_lane = lax.broadcasted_iota(jnp.int32, (span, HALF), 1) // DH
    for s in range(depth):
        query = query_ref[0, s].astype(jnp.float32)
        for h in range(GROUP):
            spread_ref[s, h * span : (h + 1) * span] = jnp.where(
                head_of_lane == h, query, 0.0
            ).astype(jnp.bfloat16)

    def bias_of(i):
        is_far, turn = table_ref[1, i], table_ref[2, i]
        lanes = pl.ds(pl.multiple_of(lax.rem(table_ref[0, i], 2) * BLOCK, BLOCK), BLOCK)
        inner = lax.rem(turn, 4)
        near = jnp.where(turn < 4, near0_ref[inner, :, :, lanes], near1_ref[inner, :, :, lanes])
        far = jnp.where(turn < 4, far0_ref[inner, :, :, lanes], far1_ref[inner, :, :, lanes])
        bias = jnp.where(is_far > 0, far, near).astype(jnp.float32)
        return (bias * LOG2E).reshape(GROUP * span, BLOCK)

    acc_ref[...] = jnp.zeros_like(acc_ref)

    def fast(t, carry):
        spots = [TILE * t + i for i in range(TILE)]
        z = [table_ref[0, i] for i in spots]
        for i in range(TILE):
            absent = jnp.where(spots[i] < live, 0.0, LOW)
            bias_ref[:, i * BLOCK : (i + 1) * BLOCK] = bias_of(spots[i]) + absent

        def weigh(s):
            keys = jnp.concatenate([key_ref[g, s, i] for i in z], axis=1)
            score = jnp.dot(spread_ref[s], keys, preferred_element_type=jnp.float32)
            return jnp.exp2(score + bias_ref[...]).astype(jnp.bfloat16)

        def add(s, weight):
            value = jnp.concatenate([value_ref[g, s, i] for i in z], axis=0)
            acc_ref[s] += jnp.dot(weight, value, preferred_element_type=jnp.float32)

        weight = weigh(0)
        for s in range(1, depth):
            later = weigh(s)
            add(s - 1, weight)
            weight = later
        add(depth - 1, weight)
        return carry

    lax.fori_loop(0, (live + TILE - 1) // TILE, fast, 0)
    totals = acc_ref[:, :, HALF:]
    bad = (live > 0) & ((jnp.max(totals) > SAFE_HIGH) | (jnp.min(totals) < SAFE_LOW))
    shift_ref[...] = jnp.zeros_like(shift_ref)

    @pl.when(bad)
    def _():
        top_ref[...] = jnp.full_like(top_ref, LOW)
        acc_ref[...] = jnp.zeros_like(acc_ref)

        def careful(t, carry):
            z = table_ref[0, t]
            bias_ref[:, :BLOCK] = bias_of(t)

            def one(s, inner):
                score = (
                    jnp.dot(spread_ref[s], key_ref[g, s, z], preferred_element_type=jnp.float32)
                    + bias_ref[:, :BLOCK]
                )
                old = top_ref[s]
                top = jnp.maximum(old, jnp.max(score, axis=1, keepdims=True))
                top_ref[s] = top
                weight = jnp.exp2(score - top).astype(jnp.bfloat16)
                acc_ref[s] = acc_ref[s] * jnp.exp2(old - top) + jnp.dot(
                    weight, value_ref[g, s, z], preferred_element_type=jnp.float32
                )
                return inner

            return lax.fori_loop(0, depth, one, carry)

        lax.fori_loop(0, live, careful, 0)
        for s in range(depth):
            shift = jnp.zeros((span, HALF), jnp.float32)
            for h in range(GROUP):
                shift = jnp.where(head_of_lane == h, top_ref[s, h * span : (h + 1) * span], shift)
            shift_ref[s] = shift

    for s in range(depth):
        total = jnp.zeros((span, HALF), jnp.float32)
        summed = jnp.zeros((span, HALF), jnp.float32)
        for h in range(GROUP):
            part = slice(h * span, (h + 1) * span)
            mine = head_of_lane == h
            summed = jnp.where(mine, acc_ref[s, part, :HALF], summed)
            total = jnp.where(mine, acc_ref[s, part, HALF:], total)
        some = total > 0.0
        safe = jnp.where(some, total, 1.0)
        mean = summed / safe
        wide = jnp.where(some, shift_ref[s] + jnp.log2(safe), LOW).T
        lse = jnp.concatenate([wide[h * DH : h * DH + 1] for h in range(GROUP)], axis=0)

        @pl.when(r == 0)
        def _():
            first = lse.astype(jnp.bfloat16).astype(jnp.float32)
            second = (lse - first).astype(jnp.bfloat16).astype(jnp.float32)
            third = lse - first - second
            sent_ref[s, :span] = mean.astype(jnp.bfloat16)
            sent_ref[s, span:] = jnp.concatenate(
                [first, second, third, jnp.zeros_like(lse)], axis=0
            ).astype(jnp.bfloat16)

        @pl.when(r == 1)
        def _():
            own_ref[s, :span] = mean
            own_ref[s, span:] = jnp.concatenate([lse, jnp.zeros_like(lse)], axis=0)


def attend(mask, rows, key_w, value_w, queries, near0, near1, far0, far1):
    blocks, depth, span, width = rows.shape
    turns = near0.shape[0]
    whole = lambda *shape: pl.BlockSpec(
        shape, lambda g, r: (0,) * len(shape), pipeline_mode=pl.Buffered(1)
    )
    bias = pl.BlockSpec((turns, GROUP, span, 2 * BLOCK), lambda g, r: (0, g, 0, 0))
    by_group = lambda g, r: (0, 0, g)
    return pl.pallas_call(
        attend_kernel,
        grid=(2, 2),
        in_specs=[
            pl.BlockSpec(memory_space=pltpu.SMEM),
            whole(blocks, depth, span, width),
            whole(width, width),
            whole(width, width),
            pl.BlockSpec((1, depth, span, HALF), lambda g, r: (r, 0, 0, g)),
            bias,
            bias,
            bias,
            bias,
        ],
        out_specs=[
            pl.BlockSpec((depth, span + EXTRA, HALF), by_group),
            pl.BlockSpec((depth, span + 8, HALF), by_group),
        ],
        out_shape=[
            jax.ShapeDtypeStruct((depth, span + EXTRA, width), jnp.bfloat16),
            jax.ShapeDtypeStruct((depth, span + 8, width), jnp.float32),
        ],
        scratch_shapes=[
            pltpu.SMEM((3, blocks), jnp.int32),
            pltpu.VMEM((2, depth, blocks, HALF, span), jnp.bfloat16),
            pltpu.VMEM((2, depth, blocks, span, 2 * HALF), jnp.bfloat16),
            pltpu.VMEM((depth, GROUP * span, HALF), jnp.bfloat16),
            pltpu.VMEM((GROUP * span, TILE * BLOCK), jnp.float32),
            pltpu.VMEM((depth, GROUP * span, 2 * HALF), jnp.float32),
            pltpu.VMEM((depth, GROUP * span, 1), jnp.float32),
            pltpu.VMEM((depth, span, HALF), jnp.float32),
        ],
        compiler_params=pltpu.CompilerParams(vmem_limit_bytes=56 * 1024 * 1024),
        name="attend",
    )(mask, rows, key_w, value_w, queries, near0, near1, far0, far1)


def finish_kernel(own_ref, got_ref, gate_ref, out_w_ref, out_off_ref, out_ref):
    depth, span, width = gate_ref.shape

    def widen(part):
        return jnp.broadcast_to(part[:, None, :], (GROUP, DH, span)).reshape(HALF, span).T

    for s in range(depth):
        gated = []
        for g in range(2):
            lanes = slice(g * HALF, (g + 1) * HALF)
            own_lse = own_ref[s, span : span + GROUP, lanes]
            pieces = got_ref[s, span:, lanes].astype(jnp.float32)
            got_lse = pieces[:GROUP] + pieces[GROUP : 2 * GROUP] + pieces[2 * GROUP : 3 * GROUP]
            own_part = widen(1.0 / (1.0 + jnp.exp2(got_lse - own_lse)))
            got_part = widen(1.0 / (1.0 + jnp.exp2(own_lse - got_lse)))
            attended = (
                own_ref[s, :span, lanes] * own_part
                + got_ref[s, :span, lanes].astype(jnp.float32) * got_part
            )
            gated.append((gate_ref[s, :, lanes] * attended).astype(jnp.bfloat16))
        result = jnp.dot(
            jnp.concatenate(gated, axis=1), out_w_ref[...], preferred_element_type=jnp.float32
        )
        out_ref[s] = (result + out_off_ref[...]).astype(jnp.bfloat16)


def finish(own, got, gate, out_w, out_off):
    return pl.pallas_call(
        finish_kernel,
        out_shape=jax.ShapeDtypeStruct(gate.shape, jnp.bfloat16),
        name="finish",
    )(own, got, gate, out_w, out_off)


def on_device(
    alignment_features,
    coupling_logit_offset,
    contact_tile_filter,
    standard_scale_array,
    standard_offset_array,
    probe_projection,
    lookup_projection,
    content_projection,
    sigmoid_projection,
    sigmoid_offset_array,
    result_projection,
    result_offset,
):
    scale, offset = standard_scale_array[None, :], standard_offset_array[None, :]
    partner = lax.ppermute(alignment_features, "res", YL_PAIRS)
    normed = normalize(alignment_features, scale, offset)
    gathered = lax.all_gather(normed, "res", axis_index_groups=Z_GROUPS)
    rounds = [
        lax.ppermute(coupling_logit_offset, ("seq", "res"), bias_pairs(u, v))
        for u in range(4)
        for v in range(2)
    ]
    near0, near1 = jnp.stack(rounds[:4]), jnp.stack(rounds[4:])
    far0 = lax.ppermute(near0, "seq", C_PAIRS)
    far1 = lax.ppermute(near1, "seq", C_PAIRS)
    queries, gate = prepare(
        normed, partner, scale, offset, probe_projection, sigmoid_projection,
        sigmoid_offset_array[None, :],
    )
    sent, own = attend(
        contact_tile_filter, gathered, lookup_projection, content_projection, queries,
        near0, near1, far0, far1,
    )
    got = lax.ppermute(sent, "res", YL_PAIRS)
    return finish(own, got, gate, result_projection, result_offset[None, :])


def solution(mesh):
    return jax.shard_map(
        on_device,
        mesh=mesh,
        in_specs=(
            P("seq", "res", None),
            P(None, "res", "seq"),
            P(),
            P(),
            P(),
            P(),
            P(),
            P(),
            P(),
            P(),
            P(),
            P(),
        ),
        out_specs=P("seq", "res", None),
        check_vma=False,
    )
```

```python
import jax
import jax.numpy as jnp
import numpy as np
from jax import lax
from jax.experimental import pallas as pl
from jax.experimental.pallas import tpu as pltpu
from jax.sharding import PartitionSpec as P

H = 8
DH = 32
BLOCK = 128
HALF = 128
GROUP = 4
TILE = 4
EXTRA = 16
SAFE_LOW = 2.0**-60
SAFE_HIGH = 2.0**90
LOG2E = 1.4426950408889634
LOW = -1e30

SEQ, RES, NZ = 16, 32, 16
Z_GROUPS = [[yl * NZ + z for z in range(NZ)] for yl in range(2)]
YL_PAIRS = [(r, (r + NZ) % RES) for r in range(RES)]
C_PAIRS = [(s, s ^ 1) for s in range(SEQ)]


def bias_pairs(u, v):
    pairs = []
    for x in range(4):
        for yh in range(2):
            for c in range(2):
                for yl in range(2):
                    for z in range(NZ):
                        to_x, to_yh, to_yl = (x + 2 * yl + u) % 4, yh ^ v, x // 2
                        source = (x * 4 + yh * 2 + c) * RES + yl * NZ + z
                        target = (to_x * 4 + to_yh * 2 + c) * RES + to_yl * NZ + z
                        pairs.append((source, target))
    return pairs


def standardize_features(source, scale, offset):
    values_f = source.astype(jnp.float32)
    center = jnp.mean(values_f, axis=-1, keepdims=True)
    spread = jnp.mean((values_f - center) ** 2, axis=-1, keepdims=True)
    return (values_f - center) * lax.rsqrt(spread + 1e-05) * scale + offset


def normalize_kernel(features_ref, scale_ref, offset_ref, out_ref):
    for s in range(features_ref.shape[0]):
        out_ref[s] = standardize_features(
            features_ref[s], scale_ref[...], offset_ref[...]
        ).astype(jnp.bfloat16)


def normalize(features, scale, offset):
    return pl.pallas_call(
        normalize_kernel,
        out_shape=jax.ShapeDtypeStruct(features.shape, jnp.bfloat16),
        name="normalize",
    )(features, scale, offset)


def prepare_kernel(
    normed_ref, partner_ref, scale_ref, offset_ref, query_w_ref, key_w_ref, gate_w_ref, gate_off_ref,
    query_ref, gate_ref,
):
    depth, span, width = normed_ref.shape
    key_wt = key_w_ref[...].astype(jnp.float32).T.astype(jnp.bfloat16)
    head_of_lane = lax.broadcasted_iota(jnp.int32, (span, HALF), 1) // DH
    for s in range(depth):
        own = normed_ref[s]
        other = standardize_features(partner_ref[s], scale_ref[...], offset_ref[...]).astype(
            jnp.bfloat16
        )
        for r, rows in enumerate((other, own)):
            query = jnp.dot(rows, query_w_ref[...], preferred_element_type=jnp.float32)
            query = query * (LOG2E / DH**0.5)
            for g in range(2):
                lanes = slice(g * HALF, (g + 1) * HALF)
                spread = jnp.concatenate(
                    [jnp.where(head_of_lane == h, query[:, lanes], 0.0) for h in range(GROUP)],
                    axis=0,
                ).astype(jnp.bfloat16)
                query_ref[r, g, s] = jnp.dot(
                    spread, key_wt[lanes], preferred_element_type=jnp.float32
                ).astype(jnp.bfloat16)
        gate_ref[s] = jax.nn.sigmoid(
            jnp.dot(own, gate_w_ref[...], preferred_element_type=jnp.float32) + gate_off_ref[...]
        )


def prepare(normed, partner, scale, offset, query_w, key_w, gate_w, gate_off):
    depth, span, width = normed.shape
    return pl.pallas_call(
        prepare_kernel,
        out_shape=[
            jax.ShapeDtypeStruct((2, 2, depth, GROUP * span, width), jnp.bfloat16),
            jax.ShapeDtypeStruct((depth, span, width), jnp.float32),
        ],
        compiler_params=pltpu.CompilerParams(vmem_limit_bytes=24 * 1024 * 1024),
        name="prepare",
    )(normed, partner, scale, offset, query_w, key_w, gate_w, gate_off)


def attend_kernel(
    mask_ref, rows_ref, value_w_ref, query_ref, near0_ref, near1_ref, far0_ref, far1_ref,
    sent_ref, own_ref,
    table_ref, bias_ref, acc_ref, sum_ref, top_ref,
):
    blocks, depth, span, width = rows_ref.shape
    g, r = pl.program_id(0), pl.program_id(1)
    seq, res = lax.axis_index("seq"), lax.axis_index("res")
    x, yh, c = seq // 4, lax.rem(seq // 2, 2), lax.rem(seq, 2)
    half, z_own = res // NZ, lax.rem(res, NZ)
    yl = jnp.where(r == 0, 1 - half, half)

    def clear(i, carry):
        for row in range(3):
            table_ref[row, i] = 0
        return carry

    def place(z, count):
        slot = z // 8 + 2 * yl
        table_ref[0, count] = z
        table_ref[1, count] = lax.rem(z // 2, 2) ^ c
        table_ref[2, count] = 2 * lax.rem(x - 2 * half - slot + 8, 4) + (lax.rem(z // 4, 2) ^ yh)
        return count + jnp.where(mask_ref[yl * NZ + z_own, half * NZ + z] > 0, 1, 0)

    lax.fori_loop(0, blocks, clear, 0)
    live = lax.fori_loop(0, blocks, place, 0)

    def bias_of(i):
        is_far, turn = table_ref[1, i], table_ref[2, i]
        lanes = pl.ds(pl.multiple_of(lax.rem(table_ref[0, i], 2) * BLOCK, BLOCK), BLOCK)
        inner = lax.rem(turn, 4)
        near = jnp.where(turn < 4, near0_ref[inner, :, :, lanes], near1_ref[inner, :, :, lanes])
        far = jnp.where(turn < 4, far0_ref[inner, :, :, lanes], far1_ref[inner, :, :, lanes])
        bias = jnp.where(is_far > 0, far, near).astype(jnp.float32)
        return (bias * LOG2E).reshape(GROUP * span, BLOCK)

    acc_ref[...] = jnp.zeros_like(acc_ref)
    sum_ref[...] = jnp.zeros_like(sum_ref)

    def scores(s, rows):
        return lax.dot_general(
            query_ref[0, 0, s], rows, (((1,), (1,)), ((), ())), preferred_element_type=jnp.float32
        )

    def tile(start, size, partial):
        spots = [start + i for i in range(size)]
        z = [table_ref[0, i] for i in spots]
        for i in range(size):
            bias = bias_of(spots[i])
            if partial:
                bias = bias + jnp.where(spots[i] < live, 0.0, LOW)
            bias_ref[:, i * BLOCK : (i + 1) * BLOCK] = bias

        def weigh(s):
            rows = jnp.concatenate([rows_ref[i, s] for i in z], axis=0)
            weight = jnp.exp2(scores(s, rows) + bias_ref[:, : size * BLOCK])
            part = weight[:, :BLOCK]
            for i in range(1, size):
                part = part + weight[:, i * BLOCK : (i + 1) * BLOCK]
            sum_ref[s] += part
            return weight.astype(jnp.bfloat16)

        def add(s, weight):
            rows = jnp.concatenate([rows_ref[i, s] for i in z], axis=0)
            acc_ref[s] += jnp.dot(weight, rows, preferred_element_type=jnp.float32)

        weight = weigh(0)
        for s in range(1, depth):
            later = weigh(s)
            add(s - 1, weight)
            weight = later
        add(depth - 1, weight)

    def full(t, carry):
        tile(TILE * t, TILE, False)
        return carry

    rest = lax.rem(live, TILE)
    lax.fori_loop(0, live // TILE, full, 0)

    @pl.when(rest > 2)
    def _():
        tile(live - rest, TILE, True)

    @pl.when((rest > 0) & (rest <= 2))
    def _():
        tile(live - rest, 2, True)

    largest, least = 0.0, SAFE_HIGH
    for s in range(depth):
        total = jnp.sum(sum_ref[s], axis=1, keepdims=True)
        sum_ref[s] = jnp.broadcast_to(total, (GROUP * span, BLOCK))
        largest = jnp.maximum(largest, jnp.max(total))
        least = jnp.minimum(least, jnp.min(total))
        top_ref[s] = jnp.zeros_like(total)
    bad = (live > 0) & ((largest > SAFE_HIGH) | (least < SAFE_LOW))

    @pl.when(bad)
    def _():
        top_ref[...] = jnp.full_like(top_ref, LOW)
        acc_ref[...] = jnp.zeros_like(acc_ref)
        sum_ref[...] = jnp.zeros_like(sum_ref)

        def careful(t, carry):
            z = table_ref[0, t]
            bias_ref[:, :BLOCK] = bias_of(t)

            def one(s, inner):
                score = scores(s, rows_ref[z, s]) + bias_ref[:, :BLOCK]
                old = top_ref[s]
                top = jnp.maximum(old, jnp.max(score, axis=1, keepdims=True))
                top_ref[s] = top
                weight = jnp.exp2(score - top)
                shrink = jnp.exp2(old - top)
                sum_ref[s] = sum_ref[s] * shrink + jnp.sum(weight, axis=1, keepdims=True)
                acc_ref[s] = acc_ref[s] * shrink + jnp.dot(
                    weight.astype(jnp.bfloat16), rows_ref[z, s], preferred_element_type=jnp.float32
                )
                return inner

            return lax.fori_loop(0, depth, one, carry)

        lax.fori_loop(0, live, careful, 0)

    head_of_lane = lax.broadcasted_iota(jnp.int32, (span, HALF), 1) // DH
    for s in range(depth):
        total = sum_ref[s]
        some = total > 0.0
        safe = jnp.where(some, total, 1.0)
        lse = jnp.where(some, top_ref[s] + jnp.log2(safe), LOW)
        inverse = 1.0 / safe
        mixed = (acc_ref[s] * jnp.concatenate([inverse, inverse], axis=1)).astype(jnp.bfloat16)
        values = jnp.dot(mixed, value_w_ref[...], preferred_element_type=jnp.float32)
        mean = values[:span]
        wide = lse[:span]
        for h in range(1, GROUP):
            part = slice(h * span, (h + 1) * span)
            mean = jnp.where(head_of_lane == h, values[part], mean)
            wide = jnp.where(head_of_lane == h, lse[part], wide)
        wide = wide.T
        lse = jnp.concatenate([wide[h * DH : h * DH + 1] for h in range(GROUP)], axis=0)

        @pl.when(r == 0)
        def _():
            first = lse.astype(jnp.bfloat16).astype(jnp.float32)
            second = (lse - first).astype(jnp.bfloat16).astype(jnp.float32)
            third = lse - first - second
            sent_ref[s, :span] = mean.astype(jnp.bfloat16)
            sent_ref[s, span:] = jnp.concatenate(
                [first, second, third, jnp.zeros_like(lse)], axis=0
            ).astype(jnp.bfloat16)

        @pl.when(r == 1)
        def _():
            own_ref[s, :span] = mean
            own_ref[s, span:] = jnp.concatenate([lse, jnp.zeros_like(lse)], axis=0)


def attend(mask, rows, value_w, queries, near0, near1, far0, far1):
    blocks, depth, span, width = rows.shape
    turns = near0.shape[0]
    bias = pl.BlockSpec((turns, GROUP, span, 2 * BLOCK), lambda g, r: (0, g, 0, 0))
    by_group = lambda g, r: (0, 0, g)
    return pl.pallas_call(
        attend_kernel,
        grid=(2, 2),
        in_specs=[
            pl.BlockSpec(memory_space=pltpu.SMEM),
            pl.BlockSpec(
                (blocks, depth, span, width),
                lambda g, r: (0, 0, 0, 0),
                pipeline_mode=pl.Buffered(1),
            ),
            pl.BlockSpec((width, HALF), lambda g, r: (0, g)),
            pl.BlockSpec((1, 1, depth, GROUP * span, width), lambda g, r: (r, g, 0, 0, 0)),
            bias,
            bias,
            bias,
            bias,
        ],
        out_specs=[
            pl.BlockSpec((depth, span + EXTRA, HALF), by_group),
            pl.BlockSpec((depth, span + 8, HALF), by_group),
        ],
        out_shape=[
            jax.ShapeDtypeStruct((depth, span + EXTRA, width), jnp.bfloat16),
            jax.ShapeDtypeStruct((depth, span + 8, width), jnp.float32),
        ],
        scratch_shapes=[
            pltpu.SMEM((3, blocks), jnp.int32),
            pltpu.VMEM((GROUP * span, TILE * BLOCK), jnp.float32),
            pltpu.VMEM((depth, GROUP * span, width), jnp.float32),
            pltpu.VMEM((depth, GROUP * span, BLOCK), jnp.float32),
            pltpu.VMEM((depth, GROUP * span, 1), jnp.float32),
        ],
        compiler_params=pltpu.CompilerParams(vmem_limit_bytes=32 * 1024 * 1024),
        name="attend",
    )(mask, rows, value_w, queries, near0, near1, far0, far1)


def finish_kernel(own_ref, got_ref, gate_ref, out_w_ref, out_off_ref, out_ref):
    depth, span, width = gate_ref.shape

    def widen(part):
        return jnp.broadcast_to(part[:, None, :], (GROUP, DH, span)).reshape(HALF, span).T

    for s in range(depth):
        gated = []
        for g in range(2):
            lanes = slice(g * HALF, (g + 1) * HALF)
            own_lse = own_ref[s, span : span + GROUP, lanes]
            pieces = got_ref[s, span:, lanes].astype(jnp.float32)
            got_lse = pieces[:GROUP] + pieces[GROUP : 2 * GROUP] + pieces[2 * GROUP : 3 * GROUP]
            own_part = widen(1.0 / (1.0 + jnp.exp2(got_lse - own_lse)))
            got_part = widen(1.0 / (1.0 + jnp.exp2(own_lse - got_lse)))
            attended = (
                own_ref[s, :span, lanes] * own_part
                + got_ref[s, :span, lanes].astype(jnp.float32) * got_part
            )
            gated.append((gate_ref[s, :, lanes] * attended).astype(jnp.bfloat16))
        result = jnp.dot(
            jnp.concatenate(gated, axis=1), out_w_ref[...], preferred_element_type=jnp.float32
        )
        out_ref[s] = (result + out_off_ref[...]).astype(jnp.bfloat16)


def finish(own, got, gate, out_w, out_off):
    return pl.pallas_call(
        finish_kernel,
        out_shape=jax.ShapeDtypeStruct(gate.shape, jnp.bfloat16),
        name="finish",
    )(own, got, gate, out_w, out_off)


def on_device(
    alignment_features,
    coupling_logit_offset,
    contact_tile_filter,
    standard_scale_array,
    standard_offset_array,
    probe_projection,
    lookup_projection,
    content_projection,
    sigmoid_projection,
    sigmoid_offset_array,
    result_projection,
    result_offset,
):
    scale, offset = standard_scale_array[None, :], standard_offset_array[None, :]
    partner = lax.ppermute(alignment_features, "res", YL_PAIRS)
    normed = normalize(alignment_features, scale, offset)
    gathered = lax.all_gather(normed, "res", axis_index_groups=Z_GROUPS)

    def rounds(bias, turns):
        return jnp.stack(
            [
                lax.ppermute(bias, ("seq", "res"), bias_pairs(u, v))
                for u in turns
                for v in range(2)
            ]
        )

    near0 = rounds(coupling_logit_offset, (0, 1))
    far0 = lax.ppermute(near0, "seq", C_PAIRS)
    later_bias, partner = lax.optimization_barrier((coupling_logit_offset, partner))
    near1 = rounds(later_bias, (2, 3))
    queries, gate = prepare(
        normed, partner, scale, offset, probe_projection, lookup_projection, sigmoid_projection,
        sigmoid_offset_array[None, :],
    )
    near1, queries, gate = lax.optimization_barrier((near1, queries, gate))
    far1 = lax.ppermute(near1, "seq", C_PAIRS)
    sent, own = attend(
        contact_tile_filter, gathered, content_projection, queries, near0, near1, far0, far1
    )
    got = lax.ppermute(sent, "res", YL_PAIRS)
    return finish(own, got, gate, result_projection, result_offset[None, :])


def solution(mesh):
    return jax.shard_map(
        on_device,
        mesh=mesh,
        in_specs=(
            P("seq", "res", None),
            P(None, "res", "seq"),
            P(),
            P(),
            P(),
            P(),
            P(),
            P(),
            P(),
            P(),
            P(),
            P(),
        ),
        out_specs=P("seq", "res", None),
        check_vma=False,
    )
```

```python
import jax
import jax.numpy as jnp
import numpy as np
from jax import lax
from jax.experimental import pallas as pl
from jax.experimental.pallas import tpu as pltpu
from jax.sharding import PartitionSpec as P

H = 8
DH = 32
BLOCK = 128
HALF = 128
GROUP = 4
TILE = 4
EXTRA = 16
SAFE_LOW = 2.0**-60
SAFE_HIGH = 2.0**90
LOG2E = 1.4426950408889634
LOW = -1e30

SEQ, RES, NZ = 16, 32, 16
Z_GROUPS = [[yl * NZ + z for z in range(NZ)] for yl in range(2)]
YL_PAIRS = [(r, (r + NZ) % RES) for r in range(RES)]
C_PAIRS = [(s, s ^ 1) for s in range(SEQ)]
PLANE_GROUPS = [[2 * k + c for k in range(SEQ // 2)] for c in range(2)]


def swap_pairs():
    pairs = []
    for x in range(4):
        for other in range(4):
            for yl in range(2):
                for z in range(NZ):
                    to_x, to_yl = (x, yl) if yl == x // 2 else ((x + 2) % 4, 1 - yl)
                    source = (x * 4 + other) * RES + yl * NZ + z
                    target = (to_x * 4 + other) * RES + to_yl * NZ + z
                    pairs.append((source, target))
    return pairs


def standardize_features(source, scale, offset):
    values_f = source.astype(jnp.float32)
    center = jnp.mean(values_f, axis=-1, keepdims=True)
    spread = jnp.mean((values_f - center) ** 2, axis=-1, keepdims=True)
    return (values_f - center) * lax.rsqrt(spread + 1e-05) * scale + offset


def normalize_kernel(features_ref, scale_ref, offset_ref, out_ref):
    for s in range(features_ref.shape[0]):
        out_ref[s] = standardize_features(
            features_ref[s], scale_ref[...], offset_ref[...]
        ).astype(jnp.bfloat16)


def normalize(features, scale, offset):
    return pl.pallas_call(
        normalize_kernel,
        out_shape=jax.ShapeDtypeStruct(features.shape, jnp.bfloat16),
        cost_estimate=pl.CostEstimate(flops=1000, bytes_accessed=1000, transcendentals=0),
        name="normalize",
    )(features, scale, offset)


def prepare_kernel(
    normed_ref, partner_ref, scale_ref, offset_ref, query_w_ref, key_w_ref, gate_w_ref, gate_off_ref,
    query_ref, gate_ref,
):
    depth, span, width = normed_ref.shape
    key_wt = key_w_ref[...].astype(jnp.float32).T.astype(jnp.bfloat16)
    head_of_lane = lax.broadcasted_iota(jnp.int32, (span, HALF), 1) // DH
    for s in range(depth):
        own = normed_ref[s]
        other = standardize_features(partner_ref[s], scale_ref[...], offset_ref[...]).astype(
            jnp.bfloat16
        )
        for r, rows in enumerate((other, own)):
            query = jnp.dot(rows, query_w_ref[...], preferred_element_type=jnp.float32)
            query = query * (LOG2E / DH**0.5)
            for g in range(2):
                lanes = slice(g * HALF, (g + 1) * HALF)
                spread = jnp.concatenate(
                    [jnp.where(head_of_lane == h, query[:, lanes], 0.0) for h in range(GROUP)],
                    axis=0,
                ).astype(jnp.bfloat16)
                query_ref[r, g, s] = jnp.dot(
                    spread, key_wt[lanes], preferred_element_type=jnp.float32
                ).astype(jnp.bfloat16)
        gate_ref[s] = jax.nn.sigmoid(
            jnp.dot(own, gate_w_ref[...], preferred_element_type=jnp.float32) + gate_off_ref[...]
        )


def prepare(normed, partner, scale, offset, query_w, key_w, gate_w, gate_off):
    depth, span, width = normed.shape
    return pl.pallas_call(
        prepare_kernel,
        out_shape=[
            jax.ShapeDtypeStruct((2, 2, depth, GROUP * span, width), jnp.bfloat16),
            jax.ShapeDtypeStruct((depth, span, width), jnp.float32),
        ],
        compiler_params=pltpu.CompilerParams(vmem_limit_bytes=24 * 1024 * 1024),
        cost_estimate=pl.CostEstimate(flops=1000, bytes_accessed=1000, transcendentals=0),
        name="prepare",
    )(normed, partner, scale, offset, query_w, key_w, gate_w, gate_off)


def attend_kernel(
    mask_ref, rows_ref, value_w_ref, query_ref, near_ref, far_ref,
    sent_ref, own_ref,
    table_ref, bias_ref, acc_ref, sum_ref, top_ref,
):
    blocks, depth, span, width = rows_ref.shape
    g, r = pl.program_id(0), pl.program_id(1)
    seq, res = lax.axis_index("seq"), lax.axis_index("res")
    c, half, z_own = lax.rem(seq, 2), res // NZ, lax.rem(res, NZ)
    yl = jnp.where(r == 0, 1 - half, half)

    def clear(i, carry):
        for row in range(3):
            table_ref[row, i] = 0
        return carry

    def place(z, count):
        holder = lax.rem(2 * half + z // 8 + jnp.where(r == 0, 2, 0), 4)
        table_ref[0, count] = z
        table_ref[1, count] = lax.rem(z // 2, 2) ^ c
        table_ref[2, count] = 2 * holder + lax.rem(z // 4, 2)
        return count + jnp.where(mask_ref[yl * NZ + z_own, half * NZ + z] > 0, 1, 0)

    lax.fori_loop(0, blocks, clear, 0)
    live = lax.fori_loop(0, blocks, place, 0)

    def bias_of(i):
        is_far, turn = table_ref[1, i], table_ref[2, i]
        lanes = pl.ds(pl.multiple_of(lax.rem(table_ref[0, i], 2) * BLOCK, BLOCK), BLOCK)
        bias = jnp.where(
            is_far > 0, far_ref[turn, :, :, lanes], near_ref[turn, :, :, lanes]
        ).astype(jnp.float32)
        return (bias * LOG2E).reshape(GROUP * span, BLOCK)

    acc_ref[...] = jnp.zeros_like(acc_ref)
    sum_ref[...] = jnp.zeros_like(sum_ref)

    def scores(s, rows):
        return lax.dot_general(
            query_ref[0, 0, s], rows, (((1,), (1,)), ((), ())), preferred_element_type=jnp.float32
        )

    def tile(start, size, partial):
        spots = [start + i for i in range(size)]
        z = [table_ref[0, i] for i in spots]
        for i in range(size):
            bias = bias_of(spots[i])
            if partial:
                bias = bias + jnp.where(spots[i] < live, 0.0, LOW)
            bias_ref[:, i * BLOCK : (i + 1) * BLOCK] = bias

        def weigh(s):
            rows = jnp.concatenate([rows_ref[i, s] for i in z], axis=0)
            weight = jnp.exp2(scores(s, rows) + bias_ref[:, : size * BLOCK])
            part = weight[:, :BLOCK]
            for i in range(1, size):
                part = part + weight[:, i * BLOCK : (i + 1) * BLOCK]
            sum_ref[s] += part
            return weight.astype(jnp.bfloat16)

        def add(s, weight):
            rows = jnp.concatenate([rows_ref[i, s] for i in z], axis=0)
            acc_ref[s] += jnp.dot(weight, rows, preferred_element_type=jnp.float32)

        weight = weigh(0)
        for s in range(1, depth):
            later = weigh(s)
            add(s - 1, weight)
            weight = later
        add(depth - 1, weight)

    def full(t, carry):
        tile(TILE * t, TILE, False)
        return carry

    rest = lax.rem(live, TILE)
    lax.fori_loop(0, live // TILE, full, 0)

    @pl.when(rest > 2)
    def _():
        tile(live - rest, TILE, True)

    @pl.when((rest > 0) & (rest <= 2))
    def _():
        tile(live - rest, 2, True)

    largest, least = 0.0, SAFE_HIGH
    for s in range(depth):
        total = jnp.sum(sum_ref[s], axis=1, keepdims=True)
        sum_ref[s] = jnp.broadcast_to(total, (GROUP * span, BLOCK))
        largest = jnp.maximum(largest, jnp.max(total))
        least = jnp.minimum(least, jnp.min(total))
        top_ref[s] = jnp.zeros_like(total)
    bad = (live > 0) & ((largest > SAFE_HIGH) | (least < SAFE_LOW))

    @pl.when(bad)
    def _():
        top_ref[...] = jnp.full_like(top_ref, LOW)
        acc_ref[...] = jnp.zeros_like(acc_ref)
        sum_ref[...] = jnp.zeros_like(sum_ref)

        def careful(t, carry):
            z = table_ref[0, t]
            bias_ref[:, :BLOCK] = bias_of(t)

            def one(s, inner):
                score = scores(s, rows_ref[z, s]) + bias_ref[:, :BLOCK]
                old = top_ref[s]
                top = jnp.maximum(old, jnp.max(score, axis=1, keepdims=True))
                top_ref[s] = top
                weight = jnp.exp2(score - top)
                shrink = jnp.exp2(old - top)
                sum_ref[s] = sum_ref[s] * shrink + jnp.sum(weight, axis=1, keepdims=True)
                acc_ref[s] = acc_ref[s] * shrink + jnp.dot(
                    weight.astype(jnp.bfloat16), rows_ref[z, s], preferred_element_type=jnp.float32
                )
                return inner

            return lax.fori_loop(0, depth, one, carry)

        lax.fori_loop(0, live, careful, 0)

    head_of_lane = lax.broadcasted_iota(jnp.int32, (span, HALF), 1) // DH
    for s in range(depth):
        total = sum_ref[s]
        some = total > 0.0
        safe = jnp.where(some, total, 1.0)
        lse = jnp.where(some, top_ref[s] + jnp.log2(safe), LOW)
        inverse = 1.0 / safe
        mixed = (acc_ref[s] * jnp.concatenate([inverse, inverse], axis=1)).astype(jnp.bfloat16)
        values = jnp.dot(mixed, value_w_ref[...], preferred_element_type=jnp.float32)
        mean = values[:span]
        wide = lse[:span]
        for h in range(1, GROUP):
            part = slice(h * span, (h + 1) * span)
            mean = jnp.where(head_of_lane == h, values[part], mean)
            wide = jnp.where(head_of_lane == h, lse[part], wide)
        wide = wide.T
        lse = jnp.concatenate([wide[h * DH : h * DH + 1] for h in range(GROUP)], axis=0)

        @pl.when(r == 0)
        def _():
            first = lse.astype(jnp.bfloat16).astype(jnp.float32)
            second = (lse - first).astype(jnp.bfloat16).astype(jnp.float32)
            third = lse - first - second
            sent_ref[s, :span] = mean.astype(jnp.bfloat16)
            sent_ref[s, span:] = jnp.concatenate(
                [first, second, third, jnp.zeros_like(lse)], axis=0
            ).astype(jnp.bfloat16)

        @pl.when(r == 1)
        def _():
            own_ref[s, :span] = mean
            own_ref[s, span:] = jnp.concatenate([lse, jnp.zeros_like(lse)], axis=0)


def attend(mask, rows, value_w, queries, near, far):
    blocks, depth, span, width = rows.shape
    turns = near.shape[0]
    bias = pl.BlockSpec((turns, GROUP, span, 2 * BLOCK), lambda g, r: (0, g, 0, 0))
    by_group = lambda g, r: (0, 0, g)
    return pl.pallas_call(
        attend_kernel,
        grid=(2, 2),
        in_specs=[
            pl.BlockSpec(memory_space=pltpu.SMEM),
            pl.BlockSpec(
                (blocks, depth, span, width),
                lambda g, r: (0, 0, 0, 0),
                pipeline_mode=pl.Buffered(1),
            ),
            pl.BlockSpec((width, HALF), lambda g, r: (0, g)),
            pl.BlockSpec((1, 1, depth, GROUP * span, width), lambda g, r: (r, g, 0, 0, 0)),
            bias,
            bias,
        ],
        out_specs=[
            pl.BlockSpec((depth, span + EXTRA, HALF), by_group),
            pl.BlockSpec((depth, span + 8, HALF), by_group),
        ],
        out_shape=[
            jax.ShapeDtypeStruct((depth, span + EXTRA, width), jnp.bfloat16),
            jax.ShapeDtypeStruct((depth, span + 8, width), jnp.float32),
        ],
        scratch_shapes=[
            pltpu.SMEM((3, blocks), jnp.int32),
            pltpu.VMEM((GROUP * span, TILE * BLOCK), jnp.float32),
            pltpu.VMEM((depth, GROUP * span, width), jnp.float32),
            pltpu.VMEM((depth, GROUP * span, BLOCK), jnp.float32),
            pltpu.VMEM((depth, GROUP * span, 1), jnp.float32),
        ],
        compiler_params=pltpu.CompilerParams(vmem_limit_bytes=56 * 1024 * 1024),
        name="attend",
    )(mask, rows, value_w, queries, near, far)


def finish_kernel(own_ref, got_ref, gate_ref, out_w_ref, out_off_ref, out_ref):
    depth, span, width = gate_ref.shape

    def widen(part):
        return jnp.broadcast_to(part[:, None, :], (GROUP, DH, span)).reshape(HALF, span).T

    for s in range(depth):
        gated = []
        for g in range(2):
            lanes = slice(g * HALF, (g + 1) * HALF)
            own_lse = own_ref[s, span : span + GROUP, lanes]
            pieces = got_ref[s, span:, lanes].astype(jnp.float32)
            got_lse = pieces[:GROUP] + pieces[GROUP : 2 * GROUP] + pieces[2 * GROUP : 3 * GROUP]
            own_part = widen(1.0 / (1.0 + jnp.exp2(got_lse - own_lse)))
            got_part = widen(1.0 / (1.0 + jnp.exp2(own_lse - got_lse)))
            attended = (
                own_ref[s, :span, lanes] * own_part
                + got_ref[s, :span, lanes].astype(jnp.float32) * got_part
            )
            gated.append((gate_ref[s, :, lanes] * attended).astype(jnp.bfloat16))
        result = jnp.dot(
            jnp.concatenate(gated, axis=1), out_w_ref[...], preferred_element_type=jnp.float32
        )
        out_ref[s] = (result + out_off_ref[...]).astype(jnp.bfloat16)


def finish(own, got, gate, out_w, out_off):
    return pl.pallas_call(
        finish_kernel,
        out_shape=jax.ShapeDtypeStruct(gate.shape, jnp.bfloat16),
        name="finish",
    )(own, got, gate, out_w, out_off)


def on_device(
    alignment_features,
    coupling_logit_offset,
    contact_tile_filter,
    standard_scale_array,
    standard_offset_array,
    probe_projection,
    lookup_projection,
    content_projection,
    sigmoid_projection,
    sigmoid_offset_array,
    result_projection,
    result_offset,
):
    scale, offset = standard_scale_array[None, :], standard_offset_array[None, :]
    partner = lax.ppermute(alignment_features, "res", YL_PAIRS)
    normed = normalize(alignment_features, scale, offset)
    gathered = lax.all_gather(normed, "res", axis_index_groups=Z_GROUPS)

    swapped = lax.ppermute(coupling_logit_offset, ("seq", "res"), swap_pairs())
    queries, gate = prepare(
        normed, partner, scale, offset, probe_projection, lookup_projection, sigmoid_projection,
        sigmoid_offset_array[None, :],
    )
    swapped, queries, gate = lax.optimization_barrier((swapped, queries, gate))
    copies = jnp.broadcast_to(swapped[None], (SEQ // 2,) + swapped.shape)
    near = lax.all_to_all(copies, "seq", 0, 0, axis_index_groups=PLANE_GROUPS, tiled=True)
    far = lax.ppermute(near, "seq", C_PAIRS)
    sent, own = attend(contact_tile_filter, gathered, content_projection, queries, near, far)
    got = lax.ppermute(sent, "res", YL_PAIRS)
    return finish(own, got, gate, result_projection, result_offset[None, :])


def solution(mesh):
    return jax.shard_map(
        on_device,
        mesh=mesh,
        in_specs=(
            P("seq", "res", None),
            P(None, "res", "seq"),
            P(),
            P(),
            P(),
            P(),
            P(),
            P(),
            P(),
            P(),
            P(),
            P(),
        ),
        out_specs=P("seq", "res", None),
        check_vma=False,
    )
```

```python
import jax
import jax.numpy as jnp
import numpy as np
from jax import lax
from jax.experimental import pallas as pl
from jax.experimental.pallas import tpu as pltpu
from jax.sharding import PartitionSpec as P

H = 8
DH = 32
BLOCK = 128
HALF = 128
GROUP = 4
TILE = 4
EXTRA = 16
SAFE_LOW = 2.0**-60
SAFE_HIGH = 2.0**90
LOG2E = 1.4426950408889634
LOW = -1e30

SEQ, RES, NZ = 16, 32, 16
Z_GROUPS = [[yl * NZ + z for z in range(NZ)] for yl in range(2)]
YL_PAIRS = [(r, (r + NZ) % RES) for r in range(RES)]
C_PAIRS = [(s, s ^ 1) for s in range(SEQ)]
PLANE_GROUPS = [[2 * k + c for k in range(SEQ // 2)] for c in range(2)]


def swap_pairs():
    pairs = []
    for x in range(4):
        for other in range(4):
            for yl in range(2):
                for z in range(NZ):
                    to_x, to_yl = (x, yl) if yl == x // 2 else ((x + 2) % 4, 1 - yl)
                    source = (x * 4 + other) * RES + yl * NZ + z
                    target = (to_x * 4 + other) * RES + to_yl * NZ + z
                    pairs.append((source, target))
    return pairs


def standardize_features(source, scale, offset):
    values_f = source.astype(jnp.float32)
    center = jnp.mean(values_f, axis=-1, keepdims=True)
    spread = jnp.mean((values_f - center) ** 2, axis=-1, keepdims=True)
    return (values_f - center) * lax.rsqrt(spread + 1e-05) * scale + offset


def normalize_kernel(features_ref, scale_ref, offset_ref, out_ref):
    for s in range(features_ref.shape[0]):
        out_ref[s] = standardize_features(
            features_ref[s], scale_ref[...], offset_ref[...]
        ).astype(jnp.bfloat16)


def normalize(features, scale, offset):
    return pl.pallas_call(
        normalize_kernel,
        out_shape=jax.ShapeDtypeStruct(features.shape, jnp.bfloat16),
        cost_estimate=pl.CostEstimate(flops=1000, bytes_accessed=1000, transcendentals=0),
        name="normalize",
    )(features, scale, offset)


def prepare_kernel(
    normed_ref, partner_ref, scale_ref, offset_ref, query_w_ref, key_w_ref, gate_w_ref, gate_off_ref,
    query_ref, gate_ref,
):
    depth, span, width = normed_ref.shape
    key_wt = key_w_ref[...].astype(jnp.float32).T.astype(jnp.bfloat16)
    head_of_lane = lax.broadcasted_iota(jnp.int32, (span, HALF), 1) // DH
    for s in range(depth):
        own = normed_ref[s]
        other = standardize_features(partner_ref[s], scale_ref[...], offset_ref[...]).astype(
            jnp.bfloat16
        )
        for r, rows in enumerate((other, own)):
            query = jnp.dot(rows, query_w_ref[...], preferred_element_type=jnp.float32)
            query = query * (LOG2E / DH**0.5)
            for g in range(2):
                lanes = slice(g * HALF, (g + 1) * HALF)
                spread = jnp.concatenate(
                    [jnp.where(head_of_lane == h, query[:, lanes], 0.0) for h in range(GROUP)],
                    axis=0,
                ).astype(jnp.bfloat16)
                query_ref[r, g, s] = jnp.dot(
                    spread, key_wt[lanes], preferred_element_type=jnp.float32
                ).astype(jnp.bfloat16)
        gate_ref[s] = jax.nn.sigmoid(
            jnp.dot(own, gate_w_ref[...], preferred_element_type=jnp.float32) + gate_off_ref[...]
        )


def prepare(normed, partner, scale, offset, query_w, key_w, gate_w, gate_off):
    depth, span, width = normed.shape
    return pl.pallas_call(
        prepare_kernel,
        out_shape=[
            jax.ShapeDtypeStruct((2, 2, depth, GROUP * span, width), jnp.bfloat16),
            jax.ShapeDtypeStruct((depth, span, width), jnp.float32),
        ],
        compiler_params=pltpu.CompilerParams(vmem_limit_bytes=24 * 1024 * 1024),
        cost_estimate=pl.CostEstimate(flops=1000, bytes_accessed=1000, transcendentals=0),
        name="prepare",
    )(normed, partner, scale, offset, query_w, key_w, gate_w, gate_off)


def attend_kernel(
    mask_ref, rows_hbm, value_w_ref, query_ref, near_hbm, far_hbm,
    sent_ref, own_ref,
    table_ref, live_ref, rows_ref, packed_ref, bias_ref, acc_ref, sum_ref, top_ref, row_sem, bias_sem,
):
    blocks, depth, span, width = rows_ref.shape
    g, r = pl.program_id(0), pl.program_id(1)
    seq, res = lax.axis_index("seq"), lax.axis_index("res")
    c, half, z_own = lax.rem(seq, 2), res // NZ, lax.rem(res, NZ)

    def is_live(line, z):
        yl = 1 - half if line == 0 else half
        return mask_ref[yl * NZ + z_own, half * NZ + z] > 0

    def row_copy(z):
        return pltpu.make_async_copy(rows_hbm.at[z], rows_ref.at[z], row_sem.at[z])

    def bias_copy(source, line, group, i, slot, spot):
        lanes = pl.ds(pl.multiple_of(lax.rem(table_ref[line, 0, i], 2) * BLOCK, BLOCK), BLOCK)
        heads = pl.ds(group * GROUP, GROUP)
        return pltpu.make_async_copy(
            source.at[table_ref[line, 2, i], heads, :, lanes],
            packed_ref.at[slot, spot],
            bias_sem.at[slot, spot],
        )

    def start_bias(line, group, i, slot, spot):
        @pl.when(table_ref[line, 1, i] > 0)
        def _():
            bias_copy(far_hbm, line, group, i, slot, spot).start()

        @pl.when(table_ref[line, 1, i] == 0)
        def _():
            bias_copy(near_hbm, line, group, i, slot, spot).start()

    def start_tile(line, group, t):
        for spot in range(TILE):
            start_bias(line, group, TILE * t + spot, lax.rem(t, 2), spot)

    @pl.when((g == 0) & (r == 0))
    def _():
        for line in range(2):

            def place(z, count):
                table_ref[line, 0, count] = z
                table_ref[line, 1, count] = lax.rem(z // 2, 2) ^ c
                holder = lax.rem(2 * half + z // 8 + (2 if line == 0 else 0), 4)
                table_ref[line, 2, count] = 2 * holder + lax.rem(z // 4, 2)
                return count + jnp.where(is_live(line, z), 1, 0)

            live = lax.fori_loop(0, blocks, place, 0)
            live_ref[line] = live

            def repeat(i, carry):
                for row in range(3):
                    table_ref[line, row, i] = table_ref[line, row, 0]
                return carry

            lax.fori_loop(live, blocks, repeat, 0)

        def needed(i, carry):
            row_copy(table_ref[0, 0, i]).start()
            return carry

        def other(z, carry):
            @pl.when(jnp.logical_not(is_live(0, z)))
            def _():
                row_copy(z).start()

            return carry

        first = jnp.minimum(live_ref[0], TILE)
        lax.fori_loop(0, first, needed, 0)

        @pl.when(live_ref[0] > 0)
        def _():
            start_tile(0, 0, 0)

        lax.fori_loop(first, live_ref[0], needed, 0)
        lax.fori_loop(0, blocks, other, 0)

    live = live_ref[r]

    acc_ref[...] = jnp.zeros_like(acc_ref)
    sum_ref[...] = jnp.zeros_like(sum_ref)

    def scores(s, rows):
        return lax.dot_general(
            query_ref[0, 0, s], rows, (((1,), (1,)), ((), ())), preferred_element_type=jnp.float32
        )

    tiles = (live + TILE - 1) // TILE

    def unpacked(slot, spot):
        return (packed_ref[slot, spot].astype(jnp.float32) * LOG2E).reshape(GROUP * span, BLOCK)

    def tile(t, size, partial):
        @pl.when(t + 1 < tiles)
        def _():
            start_tile(r, g, t + 1)

        slot = lax.rem(t, 2)
        spots = [TILE * t + i for i in range(size)]
        z = [table_ref[r, 0, i] for i in spots]

        @pl.when((g == 0) & (r == 0))
        def _():
            for i in range(size):

                @pl.when(spots[i] < live)
                def _():
                    row_copy(z[i]).wait()

        for i in range(TILE):
            bias_copy(near_hbm, r, g, TILE * t + i, slot, i).wait()
        for i in range(size):
            bias = unpacked(slot, i)
            if partial:
                bias = bias + jnp.where(spots[i] < live, 0.0, LOW)
            bias_ref[:, i * BLOCK : (i + 1) * BLOCK] = bias

        def weigh(s):
            rows = jnp.concatenate([rows_ref[i, s] for i in z], axis=0)
            weight = jnp.exp2(scores(s, rows) + bias_ref[:, : size * BLOCK])
            part = weight[:, :BLOCK]
            for i in range(1, size):
                part = part + weight[:, i * BLOCK : (i + 1) * BLOCK]
            sum_ref[s] += part
            return weight.astype(jnp.bfloat16)

        def add(s, weight):
            rows = jnp.concatenate([rows_ref[i, s] for i in z], axis=0)
            acc_ref[s] += jnp.dot(weight, rows, preferred_element_type=jnp.float32)

        weight = weigh(0)
        for s in range(1, depth):
            later = weigh(s)
            add(s - 1, weight)
            weight = later
        add(depth - 1, weight)

    def full(t, carry):
        tile(t, TILE, False)
        return carry

    rest = lax.rem(live, TILE)
    lax.fori_loop(0, live // TILE, full, 0)

    @pl.when(rest > 2)
    def _():
        tile(tiles - 1, TILE, True)

    @pl.when((rest > 0) & (rest <= 2))
    def _():
        tile(tiles - 1, 2, True)

    largest, least = 0.0, SAFE_HIGH
    for s in range(depth):
        total = jnp.sum(sum_ref[s], axis=1, keepdims=True)
        sum_ref[s] = jnp.broadcast_to(total, (GROUP * span, BLOCK))
        largest = jnp.maximum(largest, jnp.max(total))
        least = jnp.minimum(least, jnp.min(total))
        top_ref[s] = jnp.zeros_like(total)
    bad = (live > 0) & ((largest > SAFE_HIGH) | (least < SAFE_LOW))

    @pl.when(bad)
    def _():
        top_ref[...] = jnp.full_like(top_ref, LOW)
        acc_ref[...] = jnp.zeros_like(acc_ref)
        sum_ref[...] = jnp.zeros_like(sum_ref)

        def careful(t, carry):
            z = table_ref[r, 0, t]
            start_bias(r, g, t, 0, 0)
            bias_copy(near_hbm, r, g, t, 0, 0).wait()
            bias_ref[:, :BLOCK] = unpacked(0, 0)

            def one(s, inner):
                score = scores(s, rows_ref[z, s]) + bias_ref[:, :BLOCK]
                old = top_ref[s]
                top = jnp.maximum(old, jnp.max(score, axis=1, keepdims=True))
                top_ref[s] = top
                weight = jnp.exp2(score - top)
                shrink = jnp.exp2(old - top)
                sum_ref[s] = sum_ref[s] * shrink + jnp.sum(weight, axis=1, keepdims=True)
                acc_ref[s] = acc_ref[s] * shrink + jnp.dot(
                    weight.astype(jnp.bfloat16), rows_ref[z, s], preferred_element_type=jnp.float32
                )
                return inner

            return lax.fori_loop(0, depth, one, carry)

        lax.fori_loop(0, live, careful, 0)

    follower = jnp.where(r == 0, 1, 0)

    @pl.when(((g == 0) | (r == 0)) & (live_ref[follower] > 0))
    def _():
        start_tile(follower, g + r, 0)

    @pl.when((g == 0) & (r == 0))
    def _():
        def arrived(z, carry):
            @pl.when(jnp.logical_not(is_live(0, z)))
            def _():
                row_copy(z).wait()

            return carry

        lax.fori_loop(0, blocks, arrived, 0)

    head_of_lane = lax.broadcasted_iota(jnp.int32, (span, HALF), 1) // DH
    for s in range(depth):
        total = sum_ref[s]
        some = total > 0.0
        safe = jnp.where(some, total, 1.0)
        lse = jnp.where(some, top_ref[s] + jnp.log2(safe), LOW)
        inverse = 1.0 / safe
        mixed = (acc_ref[s] * jnp.concatenate([inverse, inverse], axis=1)).astype(jnp.bfloat16)
        values = jnp.dot(mixed, value_w_ref[...], preferred_element_type=jnp.float32)
        mean = values[:span]
        wide = lse[:span]
        for h in range(1, GROUP):
            part = slice(h * span, (h + 1) * span)
            mean = jnp.where(head_of_lane == h, values[part], mean)
            wide = jnp.where(head_of_lane == h, lse[part], wide)
        wide = wide.T
        lse = jnp.concatenate([wide[h * DH : h * DH + 1] for h in range(GROUP)], axis=0)

        @pl.when(r == 0)
        def _():
            first = lse.astype(jnp.bfloat16).astype(jnp.float32)
            second = (lse - first).astype(jnp.bfloat16).astype(jnp.float32)
            third = lse - first - second
            sent_ref[s, :span] = mean.astype(jnp.bfloat16)
            sent_ref[s, span:] = jnp.concatenate(
                [first, second, third, jnp.zeros_like(lse)], axis=0
            ).astype(jnp.bfloat16)

        @pl.when(r == 1)
        def _():
            own_ref[s, :span] = mean
            own_ref[s, span:] = jnp.concatenate([lse, jnp.zeros_like(lse)], axis=0)


def attend(mask, rows, value_w, queries, near, far):
    blocks, depth, span, width = rows.shape
    by_group = lambda g, r: (0, 0, g)
    return pl.pallas_call(
        attend_kernel,
        grid=(2, 2),
        in_specs=[
            pl.BlockSpec(memory_space=pltpu.SMEM),
            pl.BlockSpec(memory_space=pl.ANY),
            pl.BlockSpec((width, HALF), lambda g, r: (0, g)),
            pl.BlockSpec((1, 1, depth, GROUP * span, width), lambda g, r: (r, g, 0, 0, 0)),
            pl.BlockSpec(memory_space=pl.ANY),
            pl.BlockSpec(memory_space=pl.ANY),
        ],
        out_specs=[
            pl.BlockSpec((depth, span + EXTRA, HALF), by_group),
            pl.BlockSpec((depth, span + 8, HALF), by_group),
        ],
        out_shape=[
            jax.ShapeDtypeStruct((depth, span + EXTRA, width), jnp.bfloat16),
            jax.ShapeDtypeStruct((depth, span + 8, width), jnp.float32),
        ],
        scratch_shapes=[
            pltpu.SMEM((2, 3, blocks), jnp.int32),
            pltpu.SMEM((2,), jnp.int32),
            pltpu.VMEM((blocks, depth, span, width), jnp.bfloat16),
            pltpu.VMEM((2, TILE, GROUP, span, BLOCK), jnp.bfloat16),
            pltpu.VMEM((GROUP * span, TILE * BLOCK), jnp.float32),
            pltpu.VMEM((depth, GROUP * span, width), jnp.float32),
            pltpu.VMEM((depth, GROUP * span, BLOCK), jnp.float32),
            pltpu.VMEM((depth, GROUP * span, 1), jnp.float32),
            pltpu.SemaphoreType.DMA((blocks,)),
            pltpu.SemaphoreType.DMA((2, TILE)),
        ],
        compiler_params=pltpu.CompilerParams(vmem_limit_bytes=56 * 1024 * 1024),
        name="attend",
    )(mask, rows, value_w, queries, near, far)


def finish_kernel(own_ref, got_ref, gate_ref, out_w_ref, out_off_ref, out_ref):
    depth, span, width = gate_ref.shape

    def widen(part):
        return jnp.broadcast_to(part[:, None, :], (GROUP, DH, span)).reshape(HALF, span).T

    for s in range(depth):
        gated = []
        for g in range(2):
            lanes = slice(g * HALF, (g + 1) * HALF)
            own_lse = own_ref[s, span : span + GROUP, lanes]
            pieces = got_ref[s, span:, lanes].astype(jnp.float32)
            got_lse = pieces[:GROUP] + pieces[GROUP : 2 * GROUP] + pieces[2 * GROUP : 3 * GROUP]
            own_part = widen(1.0 / (1.0 + jnp.exp2(got_lse - own_lse)))
            got_part = widen(1.0 / (1.0 + jnp.exp2(own_lse - got_lse)))
            attended = (
                own_ref[s, :span, lanes] * own_part
                + got_ref[s, :span, lanes].astype(jnp.float32) * got_part
            )
            gated.append((gate_ref[s, :, lanes] * attended).astype(jnp.bfloat16))
        result = jnp.dot(
            jnp.concatenate(gated, axis=1), out_w_ref[...], preferred_element_type=jnp.float32
        )
        out_ref[s] = (result + out_off_ref[...]).astype(jnp.bfloat16)


def finish(own, got, gate, out_w, out_off):
    return pl.pallas_call(
        finish_kernel,
        out_shape=jax.ShapeDtypeStruct(gate.shape, jnp.bfloat16),
        name="finish",
    )(own, got, gate, out_w, out_off)


def on_device(
    alignment_features,
    coupling_logit_offset,
    contact_tile_filter,
    standard_scale_array,
    standard_offset_array,
    probe_projection,
    lookup_projection,
    content_projection,
    sigmoid_projection,
    sigmoid_offset_array,
    result_projection,
    result_offset,
):
    scale, offset = standard_scale_array[None, :], standard_offset_array[None, :]
    partner = lax.ppermute(alignment_features, "res", YL_PAIRS)
    normed = normalize(alignment_features, scale, offset)
    gathered = lax.all_gather(normed, "res", axis_index_groups=Z_GROUPS)
    swapped = lax.ppermute(coupling_logit_offset, ("seq", "res"), swap_pairs())
    swapped, partner, normed = lax.optimization_barrier((swapped, partner, normed))
    copies = jnp.broadcast_to(swapped[None], (SEQ // 2,) + swapped.shape)
    near = lax.all_to_all(copies, "seq", 0, 0, axis_index_groups=PLANE_GROUPS, tiled=True)
    far = lax.ppermute(near, "seq", C_PAIRS)
    queries, gate = prepare(
        normed, partner, scale, offset, probe_projection, lookup_projection, sigmoid_projection,
        sigmoid_offset_array[None, :],
    )
    sent, own = attend(contact_tile_filter, gathered, content_projection, queries, near, far)
    got = lax.ppermute(sent, "res", YL_PAIRS)
    return finish(own, got, gate, result_projection, result_offset[None, :])


def solution(mesh):
    return jax.shard_map(
        on_device,
        mesh=mesh,
        in_specs=(
            P("seq", "res", None),
            P(None, "res", "seq"),
            P(),
            P(),
            P(),
            P(),
            P(),
            P(),
            P(),
            P(),
            P(),
            P(),
        ),
        out_specs=P("seq", "res", None),
        check_vma=False,
    )
```

```python
import functools

import jax
import jax.numpy as jnp
import numpy as np
from jax import lax
from jax.experimental import pallas as pl
from jax.experimental.pallas import tpu as pltpu
from jax.sharding import PartitionSpec as P

H = 8
DH = 32
BLOCK = 128
HALF = 128
GROUP = 4
TILE = 4
EXTRA = 16
SAFE_LOW = 2.0**-60
SAFE_HIGH = 2.0**90
LOG2E = 1.4426950408889634
LOW = -1e30

SEQ, RES, NZ = 16, 32, 16
Z_GROUPS = [[yl * NZ + z for z in range(NZ)] for yl in range(2)]
YL_PAIRS = [(r, (r + NZ) % RES) for r in range(RES)]
C_PAIRS = [(s, s ^ 1) for s in range(SEQ)]
PLANE_GROUPS = [[2 * k + c for k in range(SEQ // 2)] for c in range(2)]


def swap_pairs():
    pairs = []
    for x in range(4):
        for other in range(4):
            for yl in range(2):
                for z in range(NZ):
                    to_x, to_yl = (x, yl) if yl == x // 2 else ((x + 2) % 4, 1 - yl)
                    source = (x * 4 + other) * RES + yl * NZ + z
                    target = (to_x * 4 + other) * RES + to_yl * NZ + z
                    pairs.append((source, target))
    return pairs


def standardize_features(source, scale, offset):
    values_f = source.astype(jnp.float32)
    center = jnp.mean(values_f, axis=-1, keepdims=True)
    spread = jnp.mean((values_f - center) ** 2, axis=-1, keepdims=True)
    return (values_f - center) * lax.rsqrt(spread + 1e-05) * scale + offset


def normalize_kernel(features_ref, scale_ref, offset_ref, out_ref):
    for s in range(features_ref.shape[0]):
        out_ref[s] = standardize_features(
            features_ref[s], scale_ref[...], offset_ref[...]
        ).astype(jnp.bfloat16)


def normalize(features, scale, offset):
    return pl.pallas_call(
        normalize_kernel,
        out_shape=jax.ShapeDtypeStruct(features.shape, jnp.bfloat16),
        cost_estimate=pl.CostEstimate(flops=1000, bytes_accessed=1000, transcendentals=0),
        name="normalize",
    )(features, scale, offset)


def prepare_kernel(
    normed_ref, partner_ref, scale_ref, offset_ref, query_w_ref, key_w_ref, gate_w_ref, gate_off_ref,
    query_ref, gate_ref,
):
    depth, span, width = normed_ref.shape
    key_wt = key_w_ref[...].astype(jnp.float32).T.astype(jnp.bfloat16)
    head_of_lane = lax.broadcasted_iota(jnp.int32, (span, HALF), 1) // DH
    for s in range(depth):
        own = normed_ref[s]
        other = standardize_features(partner_ref[s], scale_ref[...], offset_ref[...]).astype(
            jnp.bfloat16
        )
        for r, rows in enumerate((other, own)):
            query = jnp.dot(rows, query_w_ref[...], preferred_element_type=jnp.float32)
            query = query * (LOG2E / DH**0.5)
            for g in range(2):
                lanes = slice(g * HALF, (g + 1) * HALF)
                spread = jnp.concatenate(
                    [jnp.where(head_of_lane == h, query[:, lanes], 0.0) for h in range(GROUP)],
                    axis=0,
                ).astype(jnp.bfloat16)
                query_ref[r, g, s] = jnp.dot(
                    spread, key_wt[lanes], preferred_element_type=jnp.float32
                ).astype(jnp.bfloat16)
        gate_ref[s] = jax.nn.sigmoid(
            jnp.dot(own, gate_w_ref[...], preferred_element_type=jnp.float32) + gate_off_ref[...]
        )


def prepare(normed, partner, scale, offset, query_w, key_w, gate_w, gate_off):
    depth, span, width = normed.shape
    return pl.pallas_call(
        prepare_kernel,
        out_shape=[
            jax.ShapeDtypeStruct((2, 2, depth, GROUP * span, width), jnp.bfloat16),
            jax.ShapeDtypeStruct((depth, span, width), jnp.float32),
        ],
        compiler_params=pltpu.CompilerParams(vmem_limit_bytes=24 * 1024 * 1024),
        cost_estimate=pl.CostEstimate(flops=1000, bytes_accessed=1000, transcendentals=0),
        name="prepare",
    )(normed, partner, scale, offset, query_w, key_w, gate_w, gate_off)


def attend_kernel(
    own_line, mask_ref, rows_hbm, value_w_ref, query_ref, near_hbm, far_hbm,
    out_ref,
    table_ref, live_ref, rows_ref, packed_ref, bias_ref, acc_ref, sum_ref, top_ref, shift_ref, row_sem, bias_sem,
):
    blocks, depth, span, width = rows_ref.shape
    g = pl.program_id(0)
    seq, res = lax.axis_index("seq"), lax.axis_index("res")
    c, half, z_own = lax.rem(seq, 2), res // NZ, lax.rem(res, NZ)

    line = (half if own_line else 1 - half) * NZ + z_own

    def is_live(z):
        return mask_ref[line, half * NZ + z] > 0

    def row_copy(z):
        return pltpu.make_async_copy(rows_hbm.at[z], rows_ref.at[z], row_sem.at[z])

    def bias_copy(source, group, i, slot, spot):
        lanes = pl.ds(pl.multiple_of(lax.rem(table_ref[0, i], 2) * BLOCK, BLOCK), BLOCK)
        heads = pl.ds(group * GROUP, GROUP)
        return pltpu.make_async_copy(
            source.at[table_ref[2, i], heads, :, lanes],
            packed_ref.at[slot, spot],
            bias_sem.at[slot, spot],
        )

    def start_bias(group, i, slot, spot):
        @pl.when(table_ref[1, i] > 0)
        def _():
            bias_copy(far_hbm, group, i, slot, spot).start()

        @pl.when(table_ref[1, i] == 0)
        def _():
            bias_copy(near_hbm, group, i, slot, spot).start()

    def start_tile(group, t):
        for spot in range(TILE):
            start_bias(group, TILE * t + spot, lax.rem(t, 2), spot)

    @pl.when(g == 0)
    def _():
        def place(z, count):
            table_ref[0, count] = z
            table_ref[1, count] = lax.rem(z // 2, 2) ^ c
            holder = lax.rem(2 * half + z // 8 + (0 if own_line else 2), 4)
            table_ref[2, count] = 2 * holder + lax.rem(z // 4, 2)
            return count + jnp.where(is_live(z), 1, 0)

        count = lax.fori_loop(0, blocks, place, 0)
        live_ref[0] = count

        def repeat(i, carry):
            for row in range(3):
                table_ref[row, i] = table_ref[row, 0]
            return carry

        lax.fori_loop(count, blocks, repeat, 0)

        def needed(i, carry):
            row_copy(table_ref[0, i]).start()
            return carry

        first = jnp.minimum(count, TILE)
        lax.fori_loop(0, first, needed, 0)

        @pl.when(count > 0)
        def _():
            start_tile(0, 0)

        lax.fori_loop(first, count, needed, 0)

    live = live_ref[0]

    acc_ref[...] = jnp.zeros_like(acc_ref)
    sum_ref[...] = jnp.zeros_like(sum_ref)

    def scores(s, rows):
        return lax.dot_general(
            query_ref[0, 0, s], rows, (((1,), (1,)), ((), ())), preferred_element_type=jnp.float32
        )

    tiles = (live + TILE - 1) // TILE

    def unpacked(slot, spot):
        return (packed_ref[slot, spot].astype(jnp.float32) * LOG2E).reshape(GROUP * span, BLOCK)

    def tile(t, size, partial):
        @pl.when(t + 1 < tiles)
        def _():
            start_tile(g, t + 1)

        slot = lax.rem(t, 2)
        spots = [TILE * t + i for i in range(size)]
        z = [table_ref[0, i] for i in spots]

        @pl.when(g == 0)
        def _():
            for i in range(size):

                @pl.when(spots[i] < live)
                def _():
                    row_copy(z[i]).wait()

        for i in range(TILE):
            bias_copy(near_hbm, g, TILE * t + i, slot, i).wait()
        for i in range(size):
            bias = unpacked(slot, i)
            if partial:
                bias = bias + jnp.where(spots[i] < live, 0.0, LOW)
            bias_ref[:, i * BLOCK : (i + 1) * BLOCK] = bias

        def weigh(s):
            rows = jnp.concatenate([rows_ref[i, s] for i in z], axis=0)
            weight = jnp.exp2(scores(s, rows) + bias_ref[:, : size * BLOCK])
            part = weight[:, :BLOCK]
            for i in range(1, size):
                part = part + weight[:, i * BLOCK : (i + 1) * BLOCK]
            sum_ref[s] += part
            return weight.astype(jnp.bfloat16)

        def add(s, weight):
            rows = jnp.concatenate([rows_ref[i, s] for i in z], axis=0)
            acc_ref[s] += jnp.dot(weight, rows, preferred_element_type=jnp.float32)

        weight = weigh(0)
        for s in range(1, depth):
            later = weigh(s)
            add(s - 1, weight)
            weight = later
        add(depth - 1, weight)

    def full(t, carry):
        tile(t, TILE, False)
        return carry

    rest = lax.rem(live, TILE)
    lax.fori_loop(0, live // TILE, full, 0)

    @pl.when(rest > 2)
    def _():
        tile(tiles - 1, TILE, True)

    @pl.when((rest > 0) & (rest <= 2))
    def _():
        tile(tiles - 1, 2, True)

    head_of_lane = lax.broadcasted_iota(jnp.int32, (span, HALF), 1) // DH
    shift_ref[...] = jnp.zeros_like(shift_ref)
    totals = []
    for s in range(depth):
        totals.append(jnp.sum(sum_ref[s], axis=1, keepdims=True))
        sum_ref[s] = jnp.broadcast_to(totals[s], (GROUP * span, BLOCK))
    largest = jnp.max(jnp.maximum(*map(lambda p: jnp.maximum(*p), (totals[:2], totals[2:]))))
    least = jnp.min(jnp.minimum(*map(lambda p: jnp.minimum(*p), (totals[:2], totals[2:]))))
    bad = (live > 0) & ((largest > SAFE_HIGH) | (least < SAFE_LOW))

    @pl.when(bad)
    def _():
        top_ref[...] = jnp.full_like(top_ref, LOW)
        acc_ref[...] = jnp.zeros_like(acc_ref)
        sum_ref[...] = jnp.zeros_like(sum_ref)

        def careful(t, carry):
            z = table_ref[0, t]
            start_bias(g, t, 0, 0)
            bias_copy(near_hbm, g, t, 0, 0).wait()
            bias_ref[:, :BLOCK] = unpacked(0, 0)

            def one(s, inner):
                score = scores(s, rows_ref[z, s]) + bias_ref[:, :BLOCK]
                old = top_ref[s]
                top = jnp.maximum(old, jnp.max(score, axis=1, keepdims=True))
                top_ref[s] = top
                weight = jnp.exp2(score - top)
                shrink = jnp.exp2(old - top)
                sum_ref[s] = sum_ref[s] * shrink + jnp.sum(weight, axis=1, keepdims=True)
                acc_ref[s] = acc_ref[s] * shrink + jnp.dot(
                    weight.astype(jnp.bfloat16), rows_ref[z, s], preferred_element_type=jnp.float32
                )
                return inner

            return lax.fori_loop(0, depth, one, carry)

        lax.fori_loop(0, live, careful, 0)
        for s in range(depth):
            for h in range(GROUP):
                top = top_ref[s, h * span : (h + 1) * span]
                shift_ref[s] = jnp.where(head_of_lane == h, top, shift_ref[s])

    @pl.when((g == 0) & (live > 0))
    def _():
        start_tile(1, 0)

    for s in range(depth):
        values = jnp.dot(
            acc_ref[s].astype(jnp.bfloat16), value_w_ref[...], preferred_element_type=jnp.float32
        )
        mean, total = values[:span], sum_ref[s, :span]
        for h in range(1, GROUP):
            part = slice(h * span, (h + 1) * span)
            mean = jnp.where(head_of_lane == h, values[part], mean)
            total = jnp.where(head_of_lane == h, sum_ref[s, part], total)
        some = total > 0.0
        safe = jnp.where(some, total, 1.0)
        mean = mean / safe
        wide = jnp.where(some, shift_ref[s] + jnp.log2(safe), LOW).T
        lse = jnp.concatenate([wide[h * DH : h * DH + 1] for h in range(GROUP)], axis=0)

        if own_line:
            out_ref[s, :span] = mean
            out_ref[s, span:] = jnp.concatenate([lse, jnp.zeros_like(lse)], axis=0)
        else:
            first = lse.astype(jnp.bfloat16).astype(jnp.float32)
            second = (lse - first).astype(jnp.bfloat16).astype(jnp.float32)
            third = lse - first - second
            out_ref[s, :span] = mean.astype(jnp.bfloat16)
            out_ref[s, span:] = jnp.concatenate(
                [first, second, third, jnp.zeros_like(lse)], axis=0
            ).astype(jnp.bfloat16)


def attend(own_line, mask, rows, value_w, queries, near, far):
    blocks, depth, span, width = rows.shape
    r = int(own_line)
    out_rows, out_type = (span + 8, jnp.float32) if own_line else (span + EXTRA, jnp.bfloat16)
    return pl.pallas_call(
        functools.partial(attend_kernel, own_line),
        grid=(2,),
        in_specs=[
            pl.BlockSpec(memory_space=pltpu.SMEM),
            pl.BlockSpec(memory_space=pl.ANY),
            pl.BlockSpec((width, HALF), lambda g: (0, g)),
            pl.BlockSpec((1, 1, depth, GROUP * span, width), lambda g: (r, g, 0, 0, 0)),
            pl.BlockSpec(memory_space=pl.ANY),
            pl.BlockSpec(memory_space=pl.ANY),
        ],
        out_specs=pl.BlockSpec((depth, out_rows, HALF), lambda g: (0, 0, g)),
        out_shape=jax.ShapeDtypeStruct((depth, out_rows, width), out_type),
        scratch_shapes=[
            pltpu.SMEM((3, blocks), jnp.int32),
            pltpu.SMEM((1,), jnp.int32),
            pltpu.VMEM((blocks, depth, span, width), jnp.bfloat16),
            pltpu.VMEM((2, TILE, GROUP, span, BLOCK), jnp.bfloat16),
            pltpu.VMEM((GROUP * span, TILE * BLOCK), jnp.float32),
            pltpu.VMEM((depth, GROUP * span, width), jnp.float32),
            pltpu.VMEM((depth, GROUP * span, BLOCK), jnp.float32),
            pltpu.VMEM((depth, GROUP * span, 1), jnp.float32),
            pltpu.VMEM((depth, span, HALF), jnp.float32),
            pltpu.SemaphoreType.DMA((blocks,)),
            pltpu.SemaphoreType.DMA((2, TILE)),
        ],
        compiler_params=pltpu.CompilerParams(vmem_limit_bytes=56 * 1024 * 1024),
        cost_estimate=pl.CostEstimate(
            flops=8 * 10**9, bytes_accessed=10 * 2**20, transcendentals=2**23
        ),
        name="attend",
    )(mask, rows, value_w, queries, near, far)


def finish_kernel(own_ref, got_ref, gate_ref, out_w_ref, out_off_ref, out_ref):
    depth, span, width = gate_ref.shape

    def widen(part):
        return jnp.broadcast_to(part[:, None, :], (GROUP, DH, span)).reshape(HALF, span).T

    for s in range(depth):
        gated = []
        for g in range(2):
            lanes = slice(g * HALF, (g + 1) * HALF)
            own_lse = own_ref[s, span : span + GROUP, lanes]
            pieces = got_ref[s, span:, lanes].astype(jnp.float32)
            got_lse = pieces[:GROUP] + pieces[GROUP : 2 * GROUP] + pieces[2 * GROUP : 3 * GROUP]
            own_part = widen(1.0 / (1.0 + jnp.exp2(got_lse - own_lse)))
            got_part = widen(1.0 / (1.0 + jnp.exp2(own_lse - got_lse)))
            attended = (
                own_ref[s, :span, lanes] * own_part
                + got_ref[s, :span, lanes].astype(jnp.float32) * got_part
            )
            gated.append((gate_ref[s, :, lanes] * attended).astype(jnp.bfloat16))
        result = jnp.dot(
            jnp.concatenate(gated, axis=1), out_w_ref[...], preferred_element_type=jnp.float32
        )
        out_ref[s] = (result + out_off_ref[...]).astype(jnp.bfloat16)


def finish(own, got, gate, out_w, out_off):
    return pl.pallas_call(
        finish_kernel,
        out_shape=jax.ShapeDtypeStruct(gate.shape, jnp.bfloat16),
        name="finish",
    )(own, got, gate, out_w, out_off)


def on_device(
    alignment_features,
    coupling_logit_offset,
    contact_tile_filter,
    standard_scale_array,
    standard_offset_array,
    probe_projection,
    lookup_projection,
    content_projection,
    sigmoid_projection,
    sigmoid_offset_array,
    result_projection,
    result_offset,
):
    scale, offset = standard_scale_array[None, :], standard_offset_array[None, :]
    partner = lax.ppermute(alignment_features, "res", YL_PAIRS)
    normed = normalize(alignment_features, scale, offset)
    gathered = lax.all_gather(normed, "res", axis_index_groups=Z_GROUPS)
    normed, bias = lax.optimization_barrier((normed, coupling_logit_offset))
    swapped = lax.ppermute(bias, ("seq", "res"), swap_pairs())
    swapped, partner, normed = lax.optimization_barrier((swapped, partner, normed))
    copies = jnp.broadcast_to(swapped[None], (SEQ // 2,) + swapped.shape)
    near = lax.all_to_all(copies, "seq", 0, 0, axis_index_groups=PLANE_GROUPS, tiled=True)
    far = lax.ppermute(near, "seq", C_PAIRS)
    queries, gate = prepare(
        normed, partner, scale, offset, probe_projection, lookup_projection, sigmoid_projection,
        sigmoid_offset_array[None, :],
    )
    inputs = (contact_tile_filter, gathered, content_projection, queries, near, far)
    got = lax.ppermute(attend(False, *inputs), "res", YL_PAIRS)
    own = attend(True, *inputs)
    return finish(own, got, gate, result_projection, result_offset[None, :])


def solution(mesh):
    return jax.shard_map(
        on_device,
        mesh=mesh,
        in_specs=(
            P("seq", "res", None),
            P(None, "res", "seq"),
            P(),
            P(),
            P(),
            P(),
            P(),
            P(),
            P(),
            P(),
            P(),
            P(),
        ),
        out_specs=P("seq", "res", None),
        check_vma=False,
    )
```

```python
import functools

import jax
import jax.numpy as jnp
import numpy as np
from jax import lax
from jax.experimental import pallas as pl
from jax.experimental.pallas import tpu as pltpu
from jax.sharding import PartitionSpec as P

H = 8
DH = 32
BLOCK = 128
HALF = 128
GROUP = 4
TILE = 4
EXTRA = 16
SAFE_LOW = 2.0**-60
SAFE_HIGH = 2.0**90
LOG2E = 1.4426950408889634
LOW = -1e30

SEQ, RES, NZ = 16, 32, 16
Z_GROUPS = [[yl * NZ + z for z in range(NZ)] for yl in range(2)]
YL_PAIRS = [(r, (r + NZ) % RES) for r in range(RES)]
C_PAIRS = [(s, s ^ 1) for s in range(SEQ)]
PLANE_GROUPS = [[2 * k + c for k in range(SEQ // 2)] for c in range(2)]


def swap_pairs():
    pairs = []
    for x in range(4):
        for yh in range(2):
            for c in range(2):
                for yl in range(2):
                    for z in range(NZ):
                        stays = yl == x // 2
                        to = (x, yh, yl) if stays else ((x + 2) % 4, 1 - yh, 1 - yl)
                        source = (x * 4 + yh * 2 + c) * RES + yl * NZ + z
                        target = (to[0] * 4 + to[1] * 2 + c) * RES + to[2] * NZ + z
                        pairs.append((source, target))
    return pairs


def standardize_features(source, scale, offset):
    values_f = source.astype(jnp.float32)
    center = jnp.mean(values_f, axis=-1, keepdims=True)
    spread = jnp.mean((values_f - center) ** 2, axis=-1, keepdims=True)
    return (values_f - center) * lax.rsqrt(spread + 1e-05) * scale + offset


def normalize_kernel(features_ref, scale_ref, offset_ref, out_ref):
    for s in range(features_ref.shape[0]):
        out_ref[s] = standardize_features(
            features_ref[s], scale_ref[...], offset_ref[...]
        ).astype(jnp.bfloat16)


def normalize(features, scale, offset):
    return pl.pallas_call(
        normalize_kernel,
        out_shape=jax.ShapeDtypeStruct(features.shape, jnp.bfloat16),
        cost_estimate=pl.CostEstimate(flops=1000, bytes_accessed=1000, transcendentals=0),
        name="normalize",
    )(features, scale, offset)


def prepare_kernel(
    normed_ref, partner_ref, scale_ref, offset_ref, query_w_ref, key_w_ref, gate_w_ref, gate_off_ref,
    query_ref, gate_ref,
):
    depth, span, width = normed_ref.shape
    key_wt = key_w_ref[...].astype(jnp.float32).T.astype(jnp.bfloat16)
    head_of_lane = lax.broadcasted_iota(jnp.int32, (span, HALF), 1) // DH
    for s in range(depth):
        own = normed_ref[s]
        other = standardize_features(partner_ref[s], scale_ref[...], offset_ref[...]).astype(
            jnp.bfloat16
        )
        for r, rows in enumerate((other, own)):
            query = jnp.dot(rows, query_w_ref[...], preferred_element_type=jnp.float32)
            query = query * (LOG2E / DH**0.5)
            for g in range(2):
                lanes = slice(g * HALF, (g + 1) * HALF)
                spread = jnp.concatenate(
                    [jnp.where(head_of_lane == h, query[:, lanes], 0.0) for h in range(GROUP)],
                    axis=0,
                ).astype(jnp.bfloat16)
                query_ref[r, g, s] = jnp.dot(
                    spread, key_wt[lanes], preferred_element_type=jnp.float32
                ).astype(jnp.bfloat16)
        gate_ref[s] = jax.nn.sigmoid(
            jnp.dot(own, gate_w_ref[...], preferred_element_type=jnp.float32) + gate_off_ref[...]
        )


def prepare(normed, partner, scale, offset, query_w, key_w, gate_w, gate_off):
    depth, span, width = normed.shape
    return pl.pallas_call(
        prepare_kernel,
        out_shape=[
            jax.ShapeDtypeStruct((2, 2, depth, GROUP * span, width), jnp.bfloat16),
            jax.ShapeDtypeStruct((depth, span, width), jnp.float32),
        ],
        compiler_params=pltpu.CompilerParams(vmem_limit_bytes=24 * 1024 * 1024),
        cost_estimate=pl.CostEstimate(flops=1000, bytes_accessed=1000, transcendentals=0),
        name="prepare",
    )(normed, partner, scale, offset, query_w, key_w, gate_w, gate_off)


def attend_kernel(
    own_line, mask_ref, rows_hbm, value_w_ref, query_ref, near_hbm, far_hbm,
    out_ref,
    table_ref, live_ref, rows_ref, packed_ref, bias_ref, acc_ref, sum_ref, top_ref, shift_ref, row_sem, bias_sem,
):
    blocks, depth, span, width = rows_ref.shape
    g = pl.program_id(0)
    seq, res = lax.axis_index("seq"), lax.axis_index("res")
    c, half, z_own = lax.rem(seq, 2), res // NZ, lax.rem(res, NZ)

    line = (half if own_line else 1 - half) * NZ + z_own

    def is_live(z):
        return mask_ref[line, half * NZ + z] > 0

    def row_copy(z):
        return pltpu.make_async_copy(rows_hbm.at[z], rows_ref.at[z], row_sem.at[z])

    def bias_copy(source, group, i, slot, spot):
        lanes = pl.ds(pl.multiple_of(lax.rem(table_ref[0, i], 2) * BLOCK, BLOCK), BLOCK)
        heads = pl.ds(group * GROUP, GROUP)
        return pltpu.make_async_copy(
            source.at[table_ref[2, i], heads, :, lanes],
            packed_ref.at[slot, spot],
            bias_sem.at[slot, spot],
        )

    def start_bias(group, i, slot, spot):
        @pl.when(table_ref[1, i] > 0)
        def _():
            bias_copy(far_hbm, group, i, slot, spot).start()

        @pl.when(table_ref[1, i] == 0)
        def _():
            bias_copy(near_hbm, group, i, slot, spot).start()

    def start_tile(group, t):
        for spot in range(TILE):
            start_bias(group, TILE * t + spot, lax.rem(t, 2), spot)

    @pl.when(g == 0)
    def _():
        def place(z, count):
            table_ref[0, count] = z
            table_ref[1, count] = lax.rem(z // 2, 2) ^ c
            holder = lax.rem(2 * half + z // 8 + (0 if own_line else 2), 4)
            table_ref[2, count] = 2 * holder + (lax.rem(z // 4, 2) ^ (0 if own_line else 1))
            return count + jnp.where(is_live(z), 1, 0)

        count = lax.fori_loop(0, blocks, place, 0)
        live_ref[0] = count

        def repeat(i, carry):
            for row in range(3):
                table_ref[row, i] = table_ref[row, 0]
            return carry

        lax.fori_loop(count, blocks, repeat, 0)

        def needed(i, carry):
            row_copy(table_ref[0, i]).start()
            return carry

        first = jnp.minimum(count, TILE)
        lax.fori_loop(0, first, needed, 0)

        @pl.when(count > 0)
        def _():
            start_tile(0, 0)

        lax.fori_loop(first, count, needed, 0)

    live = live_ref[0]

    acc_ref[...] = jnp.zeros_like(acc_ref)
    sum_ref[...] = jnp.zeros_like(sum_ref)

    def scores(s, rows):
        return lax.dot_general(
            query_ref[0, 0, s], rows, (((1,), (1,)), ((), ())), preferred_element_type=jnp.float32
        )

    tiles = (live + TILE - 1) // TILE

    def unpacked(slot, spot):
        return (packed_ref[slot, spot].astype(jnp.float32) * LOG2E).reshape(GROUP * span, BLOCK)

    def tile(t, size, partial):
        @pl.when(t + 1 < tiles)
        def _():
            start_tile(g, t + 1)

        slot = lax.rem(t, 2)
        spots = [TILE * t + i for i in range(size)]
        z = [table_ref[0, i] for i in spots]

        @pl.when(g == 0)
        def _():
            for i in range(size):

                @pl.when(spots[i] < live)
                def _():
                    row_copy(z[i]).wait()

        for i in range(TILE):
            bias_copy(near_hbm, g, TILE * t + i, slot, i).wait()
        for i in range(size):
            bias = unpacked(slot, i)
            if partial:
                bias = bias + jnp.where(spots[i] < live, 0.0, LOW)
            bias_ref[:, i * BLOCK : (i + 1) * BLOCK] = bias

        def weigh(s):
            rows = jnp.concatenate([rows_ref[i, s] for i in z], axis=0)
            weight = jnp.exp2(scores(s, rows) + bias_ref[:, : size * BLOCK])
            part = weight[:, :BLOCK]
            for i in range(1, size):
                part = part + weight[:, i * BLOCK : (i + 1) * BLOCK]
            sum_ref[s] += part
            return weight.astype(jnp.bfloat16)

        def add(s, weight):
            rows = jnp.concatenate([rows_ref[i, s] for i in z], axis=0)
            acc_ref[s] += jnp.dot(weight, rows, preferred_element_type=jnp.float32)

        weight = weigh(0)
        for s in range(1, depth):
            later = weigh(s)
            add(s - 1, weight)
            weight = later
        add(depth - 1, weight)

    def full(t, carry):
        tile(t, TILE, False)
        return carry

    rest = lax.rem(live, TILE)
    lax.fori_loop(0, live // TILE, full, 0)

    @pl.when(rest > 2)
    def _():
        tile(tiles - 1, TILE, True)

    @pl.when((rest > 0) & (rest <= 2))
    def _():
        tile(tiles - 1, 2, True)

    head_of_lane = lax.broadcasted_iota(jnp.int32, (span, HALF), 1) // DH
    shift_ref[...] = jnp.zeros_like(shift_ref)
    totals = []
    for s in range(depth):
        totals.append(jnp.sum(sum_ref[s], axis=1, keepdims=True))
        sum_ref[s] = jnp.broadcast_to(totals[s], (GROUP * span, BLOCK))
    largest = jnp.max(jnp.maximum(*map(lambda p: jnp.maximum(*p), (totals[:2], totals[2:]))))
    least = jnp.min(jnp.minimum(*map(lambda p: jnp.minimum(*p), (totals[:2], totals[2:]))))
    bad = (live > 0) & ((largest > SAFE_HIGH) | (least < SAFE_LOW))

    @pl.when(bad)
    def _():
        top_ref[...] = jnp.full_like(top_ref, LOW)
        acc_ref[...] = jnp.zeros_like(acc_ref)
        sum_ref[...] = jnp.zeros_like(sum_ref)

        def careful(t, carry):
            z = table_ref[0, t]
            start_bias(g, t, 0, 0)
            bias_copy(near_hbm, g, t, 0, 0).wait()
            bias_ref[:, :BLOCK] = unpacked(0, 0)

            def one(s, inner):
                score = scores(s, rows_ref[z, s]) + bias_ref[:, :BLOCK]
                old = top_ref[s]
                top = jnp.maximum(old, jnp.max(score, axis=1, keepdims=True))
                top_ref[s] = top
                weight = jnp.exp2(score - top)
                shrink = jnp.exp2(old - top)
                sum_ref[s] = sum_ref[s] * shrink + jnp.sum(weight, axis=1, keepdims=True)
                acc_ref[s] = acc_ref[s] * shrink + jnp.dot(
                    weight.astype(jnp.bfloat16), rows_ref[z, s], preferred_element_type=jnp.float32
                )
                return inner

            return lax.fori_loop(0, depth, one, carry)

        lax.fori_loop(0, live, careful, 0)
        for s in range(depth):
            for h in range(GROUP):
                top = top_ref[s, h * span : (h + 1) * span]
                shift_ref[s] = jnp.where(head_of_lane == h, top, shift_ref[s])

    @pl.when((g == 0) & (live > 0))
    def _():
        start_tile(1, 0)

    for s in range(depth):
        values = jnp.dot(
            acc_ref[s].astype(jnp.bfloat16), value_w_ref[...], preferred_element_type=jnp.float32
        )
        mean, total = values[:span], sum_ref[s, :span]
        for h in range(1, GROUP):
            part = slice(h * span, (h + 1) * span)
            mean = jnp.where(head_of_lane == h, values[part], mean)
            total = jnp.where(head_of_lane == h, sum_ref[s, part], total)
        some = total > 0.0
        safe = jnp.where(some, total, 1.0)
        mean = mean / safe
        wide = jnp.where(some, shift_ref[s] + jnp.log2(safe), LOW).T
        lse = jnp.concatenate([wide[h * DH : h * DH + 1] for h in range(GROUP)], axis=0)

        if own_line:
            out_ref[s, :span] = mean
            out_ref[s, span:] = jnp.concatenate([lse, jnp.zeros_like(lse)], axis=0)
        else:
            first = lse.astype(jnp.bfloat16).astype(jnp.float32)
            second = (lse - first).astype(jnp.bfloat16).astype(jnp.float32)
            third = lse - first - second
            out_ref[s, :span] = mean.astype(jnp.bfloat16)
            out_ref[s, span:] = jnp.concatenate(
                [first, second, third, jnp.zeros_like(lse)], axis=0
            ).astype(jnp.bfloat16)


def attend(own_line, mask, rows, value_w, queries, near, far):
    blocks, depth, span, width = rows.shape
    r = int(own_line)
    out_rows, out_type = (span + 8, jnp.float32) if own_line else (span + EXTRA, jnp.bfloat16)
    return pl.pallas_call(
        functools.partial(attend_kernel, own_line),
        grid=(2,),
        in_specs=[
            pl.BlockSpec(memory_space=pltpu.SMEM),
            pl.BlockSpec(memory_space=pl.ANY),
            pl.BlockSpec((width, HALF), lambda g: (0, g)),
            pl.BlockSpec((1, 1, depth, GROUP * span, width), lambda g: (r, g, 0, 0, 0)),
            pl.BlockSpec(memory_space=pl.ANY),
            pl.BlockSpec(memory_space=pl.ANY),
        ],
        out_specs=pl.BlockSpec((depth, out_rows, HALF), lambda g: (0, 0, g)),
        out_shape=jax.ShapeDtypeStruct((depth, out_rows, width), out_type),
        scratch_shapes=[
            pltpu.SMEM((3, blocks), jnp.int32),
            pltpu.SMEM((1,), jnp.int32),
            pltpu.VMEM((blocks, depth, span, width), jnp.bfloat16),
            pltpu.VMEM((2, TILE, GROUP, span, BLOCK), jnp.bfloat16),
            pltpu.VMEM((GROUP * span, TILE * BLOCK), jnp.float32),
            pltpu.VMEM((depth, GROUP * span, width), jnp.float32),
            pltpu.VMEM((depth, GROUP * span, BLOCK), jnp.float32),
            pltpu.VMEM((depth, GROUP * span, 1), jnp.float32),
            pltpu.VMEM((depth, span, HALF), jnp.float32),
            pltpu.SemaphoreType.DMA((blocks,)),
            pltpu.SemaphoreType.DMA((2, TILE)),
        ],
        compiler_params=pltpu.CompilerParams(vmem_limit_bytes=56 * 1024 * 1024),
        cost_estimate=pl.CostEstimate(
            flops=8 * 10**9, bytes_accessed=10 * 2**20, transcendentals=2**23
        ),
        name="attend",
    )(mask, rows, value_w, queries, near, far)


def finish_kernel(own_ref, got_ref, gate_ref, out_w_ref, out_off_ref, out_ref):
    depth, span, width = gate_ref.shape

    def widen(part):
        return jnp.broadcast_to(part[:, None, :], (GROUP, DH, span)).reshape(HALF, span).T

    for s in range(depth):
        gated = []
        for g in range(2):
            lanes = slice(g * HALF, (g + 1) * HALF)
            own_lse = own_ref[s, span : span + GROUP, lanes]
            pieces = got_ref[s, span:, lanes].astype(jnp.float32)
            got_lse = pieces[:GROUP] + pieces[GROUP : 2 * GROUP] + pieces[2 * GROUP : 3 * GROUP]
            own_part = widen(1.0 / (1.0 + jnp.exp2(got_lse - own_lse)))
            got_part = widen(1.0 / (1.0 + jnp.exp2(own_lse - got_lse)))
            attended = (
                own_ref[s, :span, lanes] * own_part
                + got_ref[s, :span, lanes].astype(jnp.float32) * got_part
            )
            gated.append((gate_ref[s, :, lanes] * attended).astype(jnp.bfloat16))
        result = jnp.dot(
            jnp.concatenate(gated, axis=1), out_w_ref[...], preferred_element_type=jnp.float32
        )
        out_ref[s] = (result + out_off_ref[...]).astype(jnp.bfloat16)


def finish(own, got, gate, out_w, out_off):
    return pl.pallas_call(
        finish_kernel,
        out_shape=jax.ShapeDtypeStruct(gate.shape, jnp.bfloat16),
        name="finish",
    )(own, got, gate, out_w, out_off)


def on_device(
    alignment_features,
    coupling_logit_offset,
    contact_tile_filter,
    standard_scale_array,
    standard_offset_array,
    probe_projection,
    lookup_projection,
    content_projection,
    sigmoid_projection,
    sigmoid_offset_array,
    result_projection,
    result_offset,
):
    scale, offset = standard_scale_array[None, :], standard_offset_array[None, :]
    partner = lax.ppermute(alignment_features, "res", YL_PAIRS)
    normed = normalize(alignment_features, scale, offset)
    gathered = lax.all_gather(normed, "res", axis_index_groups=Z_GROUPS)
    swapped = lax.ppermute(coupling_logit_offset, ("seq", "res"), swap_pairs())
    swapped, partner, normed = lax.optimization_barrier((swapped, partner, normed))
    copies = jnp.broadcast_to(swapped[None], (SEQ // 2,) + swapped.shape)
    near = lax.all_to_all(copies, "seq", 0, 0, axis_index_groups=PLANE_GROUPS, tiled=True)
    far = lax.ppermute(near, "seq", C_PAIRS)
    queries, gate = prepare(
        normed, partner, scale, offset, probe_projection, lookup_projection, sigmoid_projection,
        sigmoid_offset_array[None, :],
    )
    inputs = (contact_tile_filter, gathered, content_projection, queries, near, far)
    got = lax.ppermute(attend(False, *inputs), "res", YL_PAIRS)
    own = attend(True, *inputs)
    return finish(own, got, gate, result_projection, result_offset[None, :])


def solution(mesh):
    return jax.shard_map(
        on_device,
        mesh=mesh,
        in_specs=(
            P("seq", "res", None),
            P(None, "res", "seq"),
            P(),
            P(),
            P(),
            P(),
            P(),
            P(),
            P(),
            P(),
            P(),
            P(),
        ),
        out_specs=P("seq", "res", None),
        check_vma=False,
    )
```

```python
import functools

import jax
import jax.numpy as jnp
import numpy as np
from jax import lax
from jax.experimental import pallas as pl
from jax.experimental.pallas import tpu as pltpu
from jax.sharding import PartitionSpec as P

H = 8
DH = 32
BLOCK = 128
HALF = 128
GROUP = 4
TILE = 4
EXTRA = 16
SAFE_LOW = 2.0**-60
SAFE_HIGH = 2.0**90
LOG2E = 1.4426950408889634
LOW = -1e30

SEQ, RES, NZ = 16, 32, 16
Z_GROUPS = [[yl * NZ + z for z in range(NZ)] for yl in range(2)]
YL_PAIRS = [(r, (r + NZ) % RES) for r in range(RES)]
C_PAIRS = [(s, s ^ 1) for s in range(SEQ)]
PLANE_GROUPS = [[2 * k + c for k in range(SEQ // 2)] for c in range(2)]


def swap_pairs():
    pairs = []
    for x in range(4):
        for yh in range(2):
            for c in range(2):
                for yl in range(2):
                    for z in range(NZ):
                        stays = yl == x // 2
                        to = (x, yh, yl) if stays else ((x + 2) % 4, 1 - yh, 1 - yl)
                        source = (x * 4 + yh * 2 + c) * RES + yl * NZ + z
                        target = (to[0] * 4 + to[1] * 2 + c) * RES + to[2] * NZ + z
                        pairs.append((source, target))
    return pairs


def standardize_features(source, scale, offset):
    values_f = source.astype(jnp.float32)
    center = jnp.mean(values_f, axis=-1, keepdims=True)
    spread = jnp.mean((values_f - center) ** 2, axis=-1, keepdims=True)
    return (values_f - center) * lax.rsqrt(spread + 1e-05) * scale + offset


def normalize_kernel(features_ref, scale_ref, offset_ref, out_ref):
    for s in range(features_ref.shape[0]):
        out_ref[s] = standardize_features(
            features_ref[s], scale_ref[...], offset_ref[...]
        ).astype(jnp.bfloat16)


def normalize(features, scale, offset):
    return pl.pallas_call(
        normalize_kernel,
        out_shape=jax.ShapeDtypeStruct(features.shape, jnp.bfloat16),
        cost_estimate=pl.CostEstimate(flops=1000, bytes_accessed=1000, transcendentals=0),
        name="normalize",
    )(features, scale, offset)


def prepare_kernel(
    normed_ref, partner_ref, scale_ref, offset_ref, query_w_ref, key_w_ref, gate_w_ref, gate_off_ref,
    query_ref, gate_ref,
):
    depth, span, width = normed_ref.shape
    key_wt = key_w_ref[...].astype(jnp.float32).T.astype(jnp.bfloat16)
    head_of_lane = lax.broadcasted_iota(jnp.int32, (span, HALF), 1) // DH
    for s in range(depth):
        own = normed_ref[s]
        other = standardize_features(partner_ref[s], scale_ref[...], offset_ref[...]).astype(
            jnp.bfloat16
        )
        for r, rows in enumerate((other, own)):
            query = jnp.dot(rows, query_w_ref[...], preferred_element_type=jnp.float32)
            query = query * (LOG2E / DH**0.5)
            for g in range(2):
                lanes = slice(g * HALF, (g + 1) * HALF)
                spread = jnp.concatenate(
                    [jnp.where(head_of_lane == h, query[:, lanes], 0.0) for h in range(GROUP)],
                    axis=0,
                ).astype(jnp.bfloat16)
                query_ref[r, g, s] = jnp.dot(
                    spread, key_wt[lanes], preferred_element_type=jnp.float32
                ).astype(jnp.bfloat16)
        gate_ref[s] = jax.nn.sigmoid(
            jnp.dot(own, gate_w_ref[...], preferred_element_type=jnp.float32) + gate_off_ref[...]
        )


def prepare(normed, partner, scale, offset, query_w, key_w, gate_w, gate_off):
    depth, span, width = normed.shape
    return pl.pallas_call(
        prepare_kernel,
        out_shape=[
            jax.ShapeDtypeStruct((2, 2, depth, GROUP * span, width), jnp.bfloat16),
            jax.ShapeDtypeStruct((depth, span, width), jnp.float32),
        ],
        compiler_params=pltpu.CompilerParams(vmem_limit_bytes=24 * 1024 * 1024),
        cost_estimate=pl.CostEstimate(flops=1000, bytes_accessed=1000, transcendentals=0),
        name="prepare",
    )(normed, partner, scale, offset, query_w, key_w, gate_w, gate_off)


def attend_kernel(
    own_line, mask_ref, rows_hbm, value_w_ref, query_ref, near_hbm, far_hbm,
    out_ref,
    table_ref, live_ref, rows_ref, packed_ref, bias_ref, acc_ref, sum_ref, top_ref, shift_ref, row_sem, bias_sem,
):
    blocks, depth, span, width = rows_ref.shape
    g = pl.program_id(0)
    seq, res = lax.axis_index("seq"), lax.axis_index("res")
    c, half, z_own = lax.rem(seq, 2), res // NZ, lax.rem(res, NZ)

    line = (half if own_line else 1 - half) * NZ + z_own

    def is_live(z):
        return mask_ref[line, half * NZ + z] > 0

    def row_copy(z):
        return pltpu.make_async_copy(rows_hbm.at[z], rows_ref.at[z], row_sem.at[z])

    def bias_copy(source, group, i, slot, spot):
        lanes = pl.ds(pl.multiple_of(lax.rem(table_ref[0, i], 2) * BLOCK, BLOCK), BLOCK)
        heads = pl.ds(group * GROUP, GROUP)
        return pltpu.make_async_copy(
            source.at[table_ref[2, i], heads, :, lanes],
            packed_ref.at[slot, spot],
            bias_sem.at[slot, spot],
        )

    def start_bias(group, i, slot, spot):
        @pl.when(table_ref[1, i] > 0)
        def _():
            bias_copy(far_hbm, group, i, slot, spot).start()

        @pl.when(table_ref[1, i] == 0)
        def _():
            bias_copy(near_hbm, group, i, slot, spot).start()

    def start_tile(group, t):
        for spot in range(TILE):
            start_bias(group, TILE * t + spot, lax.rem(t, 2), spot)

    @pl.when(g == 0)
    def _():
        def place(z, count):
            table_ref[0, count] = z
            table_ref[1, count] = lax.rem(z // 2, 2) ^ c
            holder = lax.rem(2 * half + z // 8 + (0 if own_line else 2), 4)
            table_ref[2, count] = 2 * holder + (lax.rem(z // 4, 2) ^ (0 if own_line else 1))
            return count + jnp.where(is_live(z), 1, 0)

        count = lax.fori_loop(0, blocks, place, 0)
        live_ref[0] = count

        def repeat(i, carry):
            for row in range(3):
                table_ref[row, i] = table_ref[row, 0]
            return carry

        lax.fori_loop(count, blocks, repeat, 0)

        def needed(i, carry):
            row_copy(table_ref[0, i]).start()
            return carry

        first = jnp.minimum(count, TILE)
        lax.fori_loop(0, first, needed, 0)

        @pl.when(count > 0)
        def _():
            start_tile(0, 0)

        lax.fori_loop(first, count, needed, 0)

    live = live_ref[0]

    acc_ref[...] = jnp.zeros_like(acc_ref)
    sum_ref[...] = jnp.zeros_like(sum_ref)

    def scores(s, rows):
        return lax.dot_general(
            query_ref[0, 0, s], rows, (((1,), (1,)), ((), ())), preferred_element_type=jnp.float32
        )

    tiles = (live + TILE - 1) // TILE

    def unpacked(slot, spot):
        return (packed_ref[slot, spot].astype(jnp.float32) * LOG2E).reshape(GROUP * span, BLOCK)

    def tile(t, size, partial):
        @pl.when(t + 1 < tiles)
        def _():
            start_tile(g, t + 1)

        slot = lax.rem(t, 2)
        spots = [TILE * t + i for i in range(size)]
        z = [table_ref[0, i] for i in spots]

        @pl.when(g == 0)
        def _():
            for i in range(size):

                @pl.when(spots[i] < live)
                def _():
                    row_copy(z[i]).wait()

        for i in range(TILE):
            bias_copy(near_hbm, g, TILE * t + i, slot, i).wait()
        for i in range(size):
            bias = unpacked(slot, i)
            if partial:
                bias = bias + jnp.where(spots[i] < live, 0.0, LOW)
            bias_ref[:, i * BLOCK : (i + 1) * BLOCK] = bias

        def weigh(s):
            rows = jnp.concatenate([rows_ref[i, s] for i in z], axis=0)
            weight = jnp.exp2(scores(s, rows) + bias_ref[:, : size * BLOCK])
            part = weight[:, :BLOCK]
            for i in range(1, size):
                part = part + weight[:, i * BLOCK : (i + 1) * BLOCK]
            sum_ref[s] += part
            return weight.astype(jnp.bfloat16)

        def add(s, weight):
            rows = jnp.concatenate([rows_ref[i, s] for i in z], axis=0)
            acc_ref[s] += jnp.dot(weight, rows, preferred_element_type=jnp.float32)

        weight = weigh(0)
        for s in range(1, depth):
            later = weigh(s)
            add(s - 1, weight)
            weight = later
        add(depth - 1, weight)

    def full(t, carry):
        tile(t, TILE, False)
        return carry

    rest = lax.rem(live, TILE)
    lax.fori_loop(0, live // TILE, full, 0)

    @pl.when(rest > 2)
    def _():
        tile(tiles - 1, TILE, True)

    @pl.when((rest > 0) & (rest <= 2))
    def _():
        tile(tiles - 1, 2, True)

    head_of_lane = lax.broadcasted_iota(jnp.int32, (span, HALF), 1) // DH
    shift_ref[...] = jnp.zeros_like(shift_ref)
    totals = []
    for s in range(depth):
        totals.append(jnp.sum(sum_ref[s], axis=1, keepdims=True))
        sum_ref[s] = jnp.broadcast_to(totals[s], (GROUP * span, BLOCK))
    largest = jnp.max(jnp.maximum(*map(lambda p: jnp.maximum(*p), (totals[:2], totals[2:]))))
    least = jnp.min(jnp.minimum(*map(lambda p: jnp.minimum(*p), (totals[:2], totals[2:]))))
    bad = (live > 0) & ((largest > SAFE_HIGH) | (least < SAFE_LOW))

    @pl.when(bad)
    def _():
        top_ref[...] = jnp.full_like(top_ref, LOW)
        acc_ref[...] = jnp.zeros_like(acc_ref)
        sum_ref[...] = jnp.zeros_like(sum_ref)

        def careful(t, carry):
            z = table_ref[0, t]
            start_bias(g, t, 0, 0)
            bias_copy(near_hbm, g, t, 0, 0).wait()
            bias_ref[:, :BLOCK] = unpacked(0, 0)

            def one(s, inner):
                score = scores(s, rows_ref[z, s]) + bias_ref[:, :BLOCK]
                old = top_ref[s]
                top = jnp.maximum(old, jnp.max(score, axis=1, keepdims=True))
                top_ref[s] = top
                weight = jnp.exp2(score - top)
                shrink = jnp.exp2(old - top)
                sum_ref[s] = sum_ref[s] * shrink + jnp.sum(weight, axis=1, keepdims=True)
                acc_ref[s] = acc_ref[s] * shrink + jnp.dot(
                    weight.astype(jnp.bfloat16), rows_ref[z, s], preferred_element_type=jnp.float32
                )
                return inner

            return lax.fori_loop(0, depth, one, carry)

        lax.fori_loop(0, live, careful, 0)
        for s in range(depth):
            for h in range(GROUP):
                top = top_ref[s, h * span : (h + 1) * span]
                shift_ref[s] = jnp.where(head_of_lane == h, top, shift_ref[s])

    @pl.when((g == 0) & (live > 0))
    def _():
        start_tile(1, 0)

    for s in range(depth):
        values = jnp.dot(
            acc_ref[s].astype(jnp.bfloat16), value_w_ref[...], preferred_element_type=jnp.float32
        )
        mean, total = values[:span], sum_ref[s, :span]
        for h in range(1, GROUP):
            part = slice(h * span, (h + 1) * span)
            mean = jnp.where(head_of_lane == h, values[part], mean)
            total = jnp.where(head_of_lane == h, sum_ref[s, part], total)
        some = total > 0.0
        safe = jnp.where(some, total, 1.0)
        mean = mean / safe
        wide = jnp.where(some, shift_ref[s] + jnp.log2(safe), LOW).T
        lse = jnp.concatenate([wide[h * DH : h * DH + 1] for h in range(GROUP)], axis=0)

        if own_line:
            out_ref[s, :span] = mean
            out_ref[s, span:] = jnp.concatenate([lse, jnp.zeros_like(lse)], axis=0)
        else:
            first = lse.astype(jnp.bfloat16).astype(jnp.float32)
            second = (lse - first).astype(jnp.bfloat16).astype(jnp.float32)
            third = lse - first - second
            out_ref[s, :span] = mean.astype(jnp.bfloat16)
            out_ref[s, span:] = jnp.concatenate(
                [first, second, third, jnp.zeros_like(lse)], axis=0
            ).astype(jnp.bfloat16)


def attend(own_line, mask, rows, value_w, queries, near, far):
    blocks, depth, span, width = rows.shape
    r = int(own_line)
    out_rows, out_type = (span + 8, jnp.float32) if own_line else (span + EXTRA, jnp.bfloat16)
    return pl.pallas_call(
        functools.partial(attend_kernel, own_line),
        grid=(2,),
        in_specs=[
            pl.BlockSpec(memory_space=pltpu.SMEM),
            pl.BlockSpec(memory_space=pl.ANY),
            pl.BlockSpec((width, HALF), lambda g: (0, g)),
            pl.BlockSpec((1, 1, depth, GROUP * span, width), lambda g: (r, g, 0, 0, 0)),
            pl.BlockSpec(memory_space=pl.ANY),
            pl.BlockSpec(memory_space=pl.ANY),
        ],
        out_specs=pl.BlockSpec((depth, out_rows, HALF), lambda g: (0, 0, g)),
        out_shape=jax.ShapeDtypeStruct((depth, out_rows, width), out_type),
        scratch_shapes=[
            pltpu.SMEM((3, blocks), jnp.int32),
            pltpu.SMEM((1,), jnp.int32),
            pltpu.VMEM((blocks, depth, span, width), jnp.bfloat16),
            pltpu.VMEM((2, TILE, GROUP, span, BLOCK), jnp.bfloat16),
            pltpu.VMEM((GROUP * span, TILE * BLOCK), jnp.float32),
            pltpu.VMEM((depth, GROUP * span, width), jnp.float32),
            pltpu.VMEM((depth, GROUP * span, BLOCK), jnp.float32),
            pltpu.VMEM((depth, GROUP * span, 1), jnp.float32),
            pltpu.VMEM((depth, span, HALF), jnp.float32),
            pltpu.SemaphoreType.DMA((blocks,)),
            pltpu.SemaphoreType.DMA((2, TILE)),
        ],
        compiler_params=pltpu.CompilerParams(vmem_limit_bytes=56 * 1024 * 1024),
        cost_estimate=pl.CostEstimate(
            flops=8 * 10**9, bytes_accessed=10 * 2**20, transcendentals=2**23
        ),
        name="attend",
    )(mask, rows, value_w, queries, near, far)


def finish_kernel(own_ref, got_ref, gate_ref, out_w_ref, out_off_ref, out_ref):
    depth, span, width = gate_ref.shape

    def widen(part):
        return jnp.broadcast_to(part[:, None, :], (GROUP, DH, span)).reshape(HALF, span).T

    for s in range(depth):
        gated = []
        for g in range(2):
            lanes = slice(g * HALF, (g + 1) * HALF)
            own_lse = own_ref[s, span : span + GROUP, lanes]
            pieces = got_ref[s, span:, lanes].astype(jnp.float32)
            got_lse = pieces[:GROUP] + pieces[GROUP : 2 * GROUP] + pieces[2 * GROUP : 3 * GROUP]
            own_part = widen(1.0 / (1.0 + jnp.exp2(got_lse - own_lse)))
            got_part = widen(1.0 / (1.0 + jnp.exp2(own_lse - got_lse)))
            attended = (
                own_ref[s, :span, lanes] * own_part
                + got_ref[s, :span, lanes].astype(jnp.float32) * got_part
            )
            gated.append((gate_ref[s, :, lanes] * attended).astype(jnp.bfloat16))
        result = jnp.dot(
            jnp.concatenate(gated, axis=1), out_w_ref[...], preferred_element_type=jnp.float32
        )
        out_ref[s] = (result + out_off_ref[...]).astype(jnp.bfloat16)


def finish(own, got, gate, out_w, out_off):
    return pl.pallas_call(
        finish_kernel,
        out_shape=jax.ShapeDtypeStruct(gate.shape, jnp.bfloat16),
        name="finish",
    )(own, got, gate, out_w, out_off)


def on_device(
    alignment_features,
    coupling_logit_offset,
    contact_tile_filter,
    standard_scale_array,
    standard_offset_array,
    probe_projection,
    lookup_projection,
    content_projection,
    sigmoid_projection,
    sigmoid_offset_array,
    result_projection,
    result_offset,
):
    scale, offset = standard_scale_array[None, :], standard_offset_array[None, :]
    width = alignment_features.shape[-1]
    normed = normalize(alignment_features, scale, offset)
    gathered = lax.all_gather(normed, "res", axis_index_groups=Z_GROUPS)

    def travel(operands):
        bias, features, _ = operands
        return (
            lax.ppermute(bias, ("seq", "res"), swap_pairs()),
            lax.ppermute(features, "res", YL_PAIRS),
        )

    def travel_flat(operands):
        bias, features, rows = operands
        flat = lax.ppermute(bias.reshape(-1, bias.shape[-1]), ("seq", "res"), swap_pairs())
        return flat.reshape(bias.shape), lax.ppermute(
            features.reshape(-1, width), "res", YL_PAIRS
        ).reshape(rows.shape)

    swapped, partner = lax.cond(
        contact_tile_filter[0, 0] > 0,
        travel,
        travel_flat,
        (coupling_logit_offset, alignment_features, normed),
    )
    swapped, partner, normed = lax.optimization_barrier((swapped, partner, normed))
    copies = jnp.broadcast_to(swapped[None], (SEQ // 2,) + swapped.shape)
    near = lax.all_to_all(copies, "seq", 0, 0, axis_index_groups=PLANE_GROUPS, tiled=True)
    far = lax.ppermute(near, "seq", C_PAIRS)
    queries, gate = prepare(
        normed, partner, scale, offset, probe_projection, lookup_projection, sigmoid_projection,
        sigmoid_offset_array[None, :],
    )
    inputs = (contact_tile_filter, gathered, content_projection, queries, near, far)
    got = lax.ppermute(attend(False, *inputs), "res", YL_PAIRS)
    own = attend(True, *inputs)
    return finish(own, got, gate, result_projection, result_offset[None, :])


def solution(mesh):
    return jax.shard_map(
        on_device,
        mesh=mesh,
        in_specs=(
            P("seq", "res", None),
            P(None, "res", "seq"),
            P(),
            P(),
            P(),
            P(),
            P(),
            P(),
            P(),
            P(),
            P(),
            P(),
        ),
        out_specs=P("seq", "res", None),
        check_vma=False,
    )
```
